256 devices in a mesh: slide: 8 (over x_lo, y), tile: 32 (over x_hi, z, core).
Axes of the slice: x: 4 (x_hi: 2, x_lo: 2; x = x_hi * 2 + x_lo), y: 4, z: 8, core: 2. Of those that a mesh axis runs over, the one named last changes fastest.
Arguments:
- tiles: bfloat16 [8, 1024, 64, 1024], P('slide', 'tile'), may hold values from -18 to 18
- counts: int32 [8, 32], P('slide', 'tile'), may hold values from 1 to 32, 512 in all within a row
- slide_ids: int32 [8, 1024], P('slide', 'tile'), may hold values from 0 to 3, as said below
- pooled_cot: bfloat16 [32, 1024], P('slide', 'tile'), may hold values from -6 to 6
- w_up: bfloat16 [1024, 256], replicated, may hold values from -0.1875 to 0.1875
- w_down: bfloat16 [256, 1024], replicated, may hold values from -0.375 to 0.375
- gain_up: float32 [256], replicated, may hold values from 0.25 to 1.75
- gain_down: float32 [1024], replicated, may hold values from 0.25 to 1.75
- attn_v: bfloat16 [1024, 256], replicated, may hold values from -0.375 to 0.375
- attn_u: bfloat16 [1024, 256], replicated, may hold values from -0.375 to 0.375
- attn_w: float32 [256], replicated, may hold values from -0.75 to 0.75
Outputs:
- pooled: float32 [32, 1024], P('slide')
- grad_w_up: float32 [1024, 256], replicated
- grad_w_down: float32 [256, 1024], replicated
- grad_gain_up: float32 [256], replicated
- grad_gain_down: float32 [1024], replicated
- grad_attn_v: float32 [1024, 256], replicated
- grad_attn_u: float32 [1024, 256], replicated
- grad_attn_w: float32 [256], replicated
The draws below stay inside these ranges and needn't reach their ends.
Inputs may be any that keep to these rules, and one draw needn't show every extreme that they name: In every band the counts sum to exactly 512, and some device of each band holds exactly 32. `slide_ids`: every slide of a band is named by local slot 0 of some device of that band.
All inputs are finite; a program needn't handle non-finite values.
Results may differ from the reference program's by a relative error of at most 0.0046.
The reference program's roundings to bfloat16 on the way count: a program that leaves them out, or rounds other values in their place, can miss the bound.
Values may be sent and summed in bfloat16 or wider, within the bound.
No kernel may reach another device: no remote copies, remote signals or barrier semaphores. Data moves between devices by JAX's collectives and lax.ppermute only.
A program may use at most 64 MiB of HBM per device.

```python
import math
import jax
import jax.numpy as jnp
import numpy as np
from jax import lax

FEAT = 1024
BOTTLE = 256
ATTN = 256
POS = 64
SL_DEV = 4
SLOTS = 32
TOTAL_BAND = 512
BAND_SLOTS = 1024
SLIDES = 32
N_SLIDE = 8
N_TILE = 32


def draw_tiles(key, part):
    key = jax.random.fold_in(key, 11)
    key_base, key_scale = jax.random.split(key, 2)
    shape_all = (N_SLIDE, BAND_SLOTS, POS, FEAT)
    tile_scale = jnp.exp(jax.random.uniform(key_scale, (N_SLIDE, BAND_SLOTS, 1, 1), jnp.float32, math.log(0.3), math.log(3.0)))
    base_draw = jnp.clip(jax.random.normal(key_base, shape_all, jnp.float32), -6.0, 6.0)
    return (base_draw * tile_scale).astype(jnp.bfloat16)


def draw_slide_ids(key, part):
    key = jax.random.fold_in(key, 12)
    key_base, key_shift = jax.random.split(key, 2)
    base_ids = jax.random.randint(key_base, (N_SLIDE, BAND_SLOTS), 0, SL_DEV, dtype=jnp.int32)
    shift_ids = jax.random.randint(key_shift, (N_SLIDE, 1), 0, SL_DEV, dtype=jnp.int32)
    slot_all = jnp.arange(BAND_SLOTS, dtype=jnp.int32)
    device_of = slot_all // SLOTS
    first_slot = slot_all % SLOTS == 0
    forced_ids = (device_of[None, :] + shift_ids) % SL_DEV
    return jnp.where(first_slot[None, :], forced_ids, base_ids).astype(jnp.int32)


def steps_of(own_key, extent, shards, low, top_value):
    factor_of = 1.0
    for dim, parts in shards:
        draws = jax.random.uniform(jax.random.fold_in(jax.random.fold_in(own_key, 6), dim), (parts,), jnp.float32, low / len(shards), top_value / len(shards))
        factor_of = factor_of * jnp.repeat(jnp.exp(draws), extent[dim] // parts).reshape((-1,) + (1,) * (len(extent) - 1 - dim))
    return factor_of


def profile(amount, total, bound, slope):
    portions = [(1 << 20) // math.isqrt(standing ** slope) + 1 for standing in range(2, amount + 1)]
    spare, given = total - bound - (amount - 1), [1] * (amount - 1)
    while spare > 0:
        movable = [i for i in range(amount - 1) if given[i] < bound]
        pool, left = sum([portions[i] for i in movable]), spare
        for i in movable:
            extra = min(bound - given[i], max(1, left * portions[i] // pool), spare)
            given[i] = given[i] + extra
            spare = spare - extra
    return np.array([bound] + given)


def ragged(key, number_of, total, most, slope):
    if number_of == 2:
        one = jax.random.randint(key, (), max(1, total - most), min(most, total - 1) + 1)
        return jnp.stack([one, total - one])
    lengths = jnp.asarray(profile(number_of, total, most, slope), jnp.int32)
    twos = (number_of - 1) // 2
    giver, receiver = lengths[1:1 + 2 * twos:2], lengths[2:2 + 2 * twos:2]
    slack = jnp.minimum(giver - 1, most - receiver)
    shifted = jax.random.randint(jax.random.fold_in(key, 1), (twos,), 0, 1 << 20) % (slack + 1)
    lengths = lengths.at[1:1 + 2 * twos:2].set(giver - shifted).at[2:2 + 2 * twos:2].set(receiver + shifted)
    return lengths[jax.random.permutation(jax.random.fold_in(key, 2), number_of)]


def normal_values(own_key, dims, spread, bound, cuts=(), held_as=jnp.bfloat16):
    values = jax.random.normal(own_key, dims, jnp.float32) * spread
    if len(cuts) > 0:
        values = steps_of(own_key, dims, cuts, -0.22, 0.18) * values
    return jnp.clip(values, min=-bound, max=bound).astype(held_as)


def setup_inputs(seed: int = 0) -> dict:
    key_list = jax.random.split(jax.random.key(seed), 12)
    return {
        "tiles": draw_tiles(jax.random.fold_in(key_list[11], 71), 0),
        "counts": jax.vmap(lambda own: ragged(own, N_TILE, TOTAL_BAND, SLOTS, 2))(jax.random.split(key_list[1], N_SLIDE)).reshape((N_SLIDE, N_TILE)).astype(jnp.int32),
        "slide_ids": draw_slide_ids(jax.random.fold_in(key_list[11], 71), 0),
        "pooled_cot": normal_values(key_list[3], (SLIDES, FEAT), 1.0, 6.0, ((0, 8), (1, 32))),
        "w_up": normal_values(key_list[4], (FEAT, BOTTLE), FEAT ** -0.5, 0.1875),
        "w_down": normal_values(key_list[5], (BOTTLE, FEAT), BOTTLE ** -0.5, 0.375),
        "gain_up": jnp.clip(1.0 + 0.15 * jax.random.normal(key_list[6], (BOTTLE,), jnp.float32), 0.25, 1.75),
        "gain_down": jnp.clip(1.0 + 0.15 * jax.random.normal(key_list[7], (FEAT,), jnp.float32), 0.25, 1.75),
        "attn_v": normal_values(key_list[8], (FEAT, ATTN), (FEAT // 4) ** -0.5, 0.375),
        "attn_u": normal_values(key_list[9], (FEAT, ATTN), (FEAT // 4) ** -0.5, 0.375),
        "attn_w": normal_values(key_list[10], (ATTN,), (ATTN // 4) ** -0.5, 0.75, (), jnp.float32),
    }


HIGHEST = lax.Precision.HIGHEST


def forward(tile_rows, w_up, w_down, gain_up, gain_down, attn_v, attn_u, attn_w, positions):
    up_proj = jnp.dot(tile_rows, w_up, preferred_element_type=jnp.float32)
    scaled_up = up_proj * gain_up
    hidden = jax.nn.relu(scaled_up).astype(jnp.bfloat16)
    down_proj = jnp.dot(hidden, w_down, preferred_element_type=jnp.float32)
    residual_sum = tile_rows.astype(jnp.float32) + down_proj * gain_down
    width = residual_sum.shape[-1]
    features = jnp.mean(jax.nn.relu(residual_sum).reshape(-1, positions, width), axis=1)
    features_b = features.astype(jnp.bfloat16)
    tanh_gate = jnp.tanh(jnp.dot(features_b, attn_v, preferred_element_type=jnp.float32))
    sigm_gate = jax.nn.sigmoid(jnp.dot(features_b, attn_u, preferred_element_type=jnp.float32))
    score = jnp.sum(tanh_gate * sigm_gate * attn_w, axis=-1)
    weight = jax.nn.sigmoid(score)
    return (up_proj, scaled_up, hidden, down_proj, residual_sum, features, features_b, tanh_gate, sigm_gate, weight)


def backward(tile_rows, saved_state, member, pooled, denominator, cot_full, w_up, w_down, gain_up, gain_down, attn_v, attn_u, attn_w, positions):
    up_proj, scaled_up, hidden, down_proj, residual_sum, features, features_b, tanh_gate, sigm_gate, weight = saved_state
    cot_tile = jnp.dot(member, cot_full, precision=HIGHEST)
    pooled_tile = jnp.dot(member, pooled, precision=HIGHEST)
    den_sum = jnp.sum(member * denominator[None, :], axis=1)
    den_tile = jnp.where(jnp.sum(member, axis=1) > 0.5, den_sum, 1.0)
    weight_share = weight / den_tile
    dfeatures = weight_share[:, None] * cot_tile
    dweight = jnp.sum(cot_tile * (features - pooled_tile), axis=1) / den_tile
    dscore = dweight * weight * (1.0 - weight)
    grad_attn_w = jnp.sum(dscore[:, None] * tanh_gate * sigm_gate, axis=0)
    grad_tanh = dscore[:, None] * attn_w * sigm_gate * (1.0 - tanh_gate * tanh_gate)
    grad_sigm = dscore[:, None] * attn_w * tanh_gate * sigm_gate * (1.0 - sigm_gate)
    features_f = features_b.astype(jnp.float32)
    grad_attn_v = jnp.dot(features_f.T, grad_tanh, precision=HIGHEST)
    grad_attn_u = jnp.dot(features_f.T, grad_sigm, precision=HIGHEST)
    dfeatures = dfeatures + jnp.dot(grad_tanh, attn_v.astype(jnp.float32).T, precision=HIGHEST)
    dfeatures = dfeatures + jnp.dot(grad_sigm, attn_u.astype(jnp.float32).T, precision=HIGHEST)
    tile_total = dfeatures.shape[0]
    width = dfeatures.shape[1]
    active = residual_sum.reshape(tile_total, positions, width) > 0
    dresidual = jnp.where(active, (dfeatures / positions)[:, None, :], 0.0).reshape(-1, width)
    grad_gain_down = jnp.sum(dresidual * down_proj, axis=0)
    dback = (dresidual * gain_down).astype(jnp.bfloat16)
    grad_w_down = jnp.dot(hidden.T, dback, preferred_element_type=jnp.float32)
    dhidden = jnp.dot(dback, w_down.T, preferred_element_type=jnp.float32)
    dscaled = jnp.where(scaled_up > 0, dhidden, 0.0)
    grad_gain_up = jnp.sum(dscaled * up_proj, axis=0)
    dup = (dscaled * gain_up).astype(jnp.bfloat16)
    grad_w_up = jnp.dot(tile_rows.T, dup, preferred_element_type=jnp.float32)
    return (grad_w_up, grad_w_down, grad_gain_up, grad_gain_down, grad_attn_v, grad_attn_u, grad_attn_w)


def band_tiles(tiles_band, counts_band, slide_band):
    slot_index = jnp.arange(BAND_SLOTS, dtype=jnp.int32) % SLOTS
    device_index = jnp.arange(BAND_SLOTS, dtype=jnp.int32) // SLOTS
    valid_slot = slot_index < counts_band[device_index]
    pick_rows = jnp.nonzero(valid_slot, size=TOTAL_BAND)[0].astype(jnp.int32)
    chosen = tiles_band[pick_rows]
    slide_range = jnp.arange(SL_DEV, dtype=jnp.int32)
    member = (slide_band[pick_rows][:, None] == slide_range[None, :]).astype(jnp.float32)
    return chosen.reshape(-1, FEAT), member


def reference(tiles, counts, slide_ids, pooled_cot, w_up, w_down, gain_up, gain_down, attn_v, attn_u, attn_w):
    weights_all = (w_up, w_down, gain_up, gain_down, attn_v, attn_u, attn_w)

    def pool_band(band_index):
        tile_rows, member = band_tiles(tiles[band_index], counts[band_index], slide_ids[band_index])
        saved_state = forward(tile_rows, *weights_all, POS)
        features = saved_state[5]
        weight = saved_state[9]
        numerator = jnp.dot(member.T, weight[:, None] * features, precision=HIGHEST)
        denominator = jnp.sum(member * weight[:, None], axis=0)
        return numerator, denominator

    numerators, denominators = lax.map(pool_band, jnp.arange(N_SLIDE, dtype=jnp.int32))
    pooled = numerators / denominators[:, :, None]
    cot_bands = pooled_cot.astype(jnp.float32).reshape(N_SLIDE, SL_DEV, FEAT)

    def grad_band(band_index):
        tile_rows, member = band_tiles(tiles[band_index], counts[band_index], slide_ids[band_index])
        saved_state = forward(tile_rows, *weights_all, POS)
        return backward(tile_rows, saved_state, member, pooled[band_index], denominators[band_index], cot_bands[band_index], *weights_all, POS)

    stacked = lax.map(grad_band, jnp.arange(N_SLIDE, dtype=jnp.int32))
    summed = [jnp.sum(part_grad, axis=0) for part_grad in stacked]
    return (pooled.reshape(SLIDES, FEAT), summed[0], summed[1], summed[2], summed[3], summed[4], summed[5], summed[6])
```

```python
import jax
import jax.numpy as jnp
from jax import lax
from jax.experimental import pallas as pl
from jax.experimental.pallas import tpu as pltpu
from jax.sharding import Mesh
from jax.sharding import PartitionSpec as P

F32 = jnp.float32
BF16 = jnp.bfloat16

FINE = ("x_lo", "y", "x_hi", "z", "core")
SLIDE = ("x_lo", "y")
TILE = ("x_hi", "z", "core")
PEERS = ("x_hi", "z")
PLANE = ("x_lo", "y", "x_hi")
N_PEERS = 16
N_PLANE = 16
N_Z = 8

SLOTS = 32
POS = 64
FEAT = 1024
BOT = 256
ATT = 256
LANE = 128
STEPS = 4
GROUP = SLOTS // STEPS
PIECE = 32
HALF = 16
BLOCKS = FEAT // LANE
MAIN = PIECE * BLOCKS
TALL = MAIN + HALF
ROWS = GROUP * POS

VMEM_LIMIT = 48 * 1024 * 1024


def params():
    return pltpu.CompilerParams(vmem_limit_bytes=VMEM_LIMIT)


def nn(a, b):
    return jnp.dot(a, b, preferred_element_type=F32)


def nt(a, b):
    return lax.dot_general(a, b, (((1,), (1,)), ((), ())), preferred_element_type=F32)


def tn(a, b):
    return lax.dot_general(a, b, (((0,), (0,)), ((), ())), preferred_element_type=F32)


def sigmoid(v):
    return 1.0 / (1.0 + jnp.exp(-v))


def column(row):
    n = row.shape[1]
    i = lax.broadcasted_iota(jnp.int32, (n, n), 0)
    j = lax.broadcasted_iota(jnp.int32, (n, n), 1)
    return jnp.sum(jnp.where(i == j, jnp.broadcast_to(row, (n, n)), 0), axis=1, keepdims=True)


def members(ids_ref, count):
    ids = column(ids_ref[...])
    slot = lax.broadcasted_iota(jnp.int32, (SLOTS, 1), 0)
    live = slot < count
    return [jnp.logical_and(live, ids == c) for c in range(4)], live


def split3(v):
    hi = v.astype(BF16)
    rest = v - hi.astype(F32)
    mid = rest.astype(BF16)
    low = (rest - mid.astype(F32)).astype(BF16)
    return [hi, mid, low]


def forward_kernel(
    count_ref, x_ref, ids_ref, cot_ref, wu_ref, wd_ref, gu_ref, gd_ref, av_ref, au_ref, aw_ref,
    mask_ref, hid_ref, up_ref, feat_ref, act_ref, tanh_ref, sigm_ref, weight_ref, pack_ref,
):
    step = pl.program_id(0)
    x = x_ref[...]
    up = nn(x, wu_ref[...])
    up_ref[...] = up
    hidden = jnp.maximum(up * gu_ref[...], 0.0).astype(BF16)
    hid_ref[...] = hidden
    down = nn(hidden, wd_ref[...])
    res = x.astype(F32) + down * gd_ref[...]
    positive = res > 0
    mask_ref[...] = jnp.where(positive, 1.0, 0.0).astype(BF16)
    feats = jnp.sum(jnp.maximum(res, 0.0).reshape(GROUP, POS, FEAT), axis=1) * (1.0 / POS)
    acts = jnp.sum(jnp.where(positive, down, 0.0).reshape(GROUP, POS, FEAT), axis=1)
    at = pl.ds(pl.multiple_of(step * GROUP, GROUP), GROUP)
    feat_ref[at, :] = feats
    act_ref[at, :] = acts

    @pl.when(step == STEPS - 1)
    def _():
        feat = feat_ref[...]
        feat_b = feat.astype(BF16)
        tanh = jnp.tanh(nn(feat_b, av_ref[...]))
        sigm = sigmoid(nn(feat_b, au_ref[...]))
        tanh_ref[...] = tanh
        sigm_ref[...] = sigm
        weight = sigmoid(jnp.sum(tanh * sigm * aw_ref[...], axis=1, keepdims=True))
        weight_ref[...] = jnp.broadcast_to(weight, (SLOTS, LANE))
        member, _ = members(ids_ref, count_ref[0, 0])
        for c in range(4):
            share = jnp.where(member[c], weight, 0.0)
            num = jnp.sum(share * feat, axis=0, keepdims=True)
            den = jnp.sum(share, axis=0, keepdims=True)
            for r in range(8):
                pack_ref[8 * c + r : 8 * c + r + 1, :] = num[:, LANE * r : LANE * (r + 1)]
            pack_ref[36 + c : 37 + c, :] = jnp.broadcast_to(den, (1, LANE))
        quarter = lax.rem(lax.axis_index("z"), 2) * 2 + lax.axis_index("core")
        lane = lax.broadcasted_iota(jnp.int32, (4, LANE), 1)
        mine = jnp.logical_and(lane >= quarter * 32, lane < quarter * 32 + 32)
        cot = cot_ref[...].astype(F32)
        cot = jnp.concatenate([cot, cot, cot, cot], axis=1)
        pack_ref[32:36, :] = jnp.where(mine, cot, 0.0)


def pair_kernel(mine_ref, other_ref, out_ref):
    half = lax.axis_index("core") * 16
    at = pl.ds(pl.multiple_of(half, 16), 16)
    top = mine_ref[at, :] + other_ref[at, :]
    tail = mine_ref[32:40, :] + other_ref[32:40, :]
    for p in range(N_PEERS):
        out_ref[p, 0:16, :] = top
        out_ref[p, 16:24, :] = tail


def middle_kernel(
    count_ref, ids_ref, got_ref, other_ref, feat_ref, act_ref, tanh_ref, sigm_ref, weight_ref,
    av_ref, au_ref, aw_ref, gd_ref,
    back_ref, pooled_ref, small_ref, keep_ref, send_ref,
):
    core = lax.axis_index("core")
    total = got_ref[0]
    total_o = other_ref[0, 0:16, :]
    for p in range(1, N_PEERS):
        total = total + got_ref[p]
        total_o = total_o + other_ref[p, 0:16, :]
    low = jnp.where(core == 0, total[0:16], total_o)
    high = jnp.where(core == 0, total_o, total[0:16])
    cot = jnp.concatenate(
        [got_ref[2 * b, 16:20, :] + got_ref[2 * b + 1, 16:20, :] for b in range(8)], axis=1
    )
    member, live = members(ids_ref, count_ref[0, 0])
    cot_tile = jnp.zeros((SLOTS, FEAT), F32)
    pooled_tile = jnp.zeros((SLOTS, FEAT), F32)
    den_tile = jnp.where(live, 0.0, 1.0)
    for c in range(4):
        part = (low, high)[c // 2]
        base = 8 * (c % 2)
        num = jnp.concatenate([part[base + r : base + r + 1, :] for r in range(8)], axis=1)
        den = total[20 + c : 21 + c, 0:1]
        pooled = num / den
        pooled_ref[c : c + 1, :] = pooled
        cot_tile = jnp.where(member[c], cot[c : c + 1, :], cot_tile)
        pooled_tile = jnp.where(member[c], pooled, pooled_tile)
        den_tile = jnp.where(member[c], den, den_tile)
    feat = feat_ref[...]
    tanh = tanh_ref[...]
    sigm = sigm_ref[...]
    weight = weight_ref[:, 0:1]
    aw = aw_ref[...]
    dweight = jnp.sum(cot_tile * (feat - pooled_tile), axis=1, keepdims=True) / den_tile
    dscore = dweight * weight * (1.0 - weight)
    grad_aw = jnp.sum(dscore * tanh * sigm, axis=0, keepdims=True)
    grad_t = dscore * aw * sigm * (1.0 - tanh * tanh)
    grad_s = dscore * aw * tanh * sigm * (1.0 - sigm)
    parts_t = jnp.concatenate(split3(grad_t), axis=0)
    parts_s = jnp.concatenate(split3(grad_s), axis=0)
    feat_b = feat.astype(BF16)
    feat_3 = jnp.concatenate([feat_b, feat_b, feat_b], axis=0)
    grad_v = tn(parts_t, feat_3)
    grad_u = tn(parts_s, feat_3)

    @pl.when(core == 0)
    def _():
        keep_ref[...] = grad_v
        send_ref[...] = grad_u.astype(BF16)

    @pl.when(core != 0)
    def _():
        keep_ref[...] = grad_u
        send_ref[...] = grad_v.astype(BF16)

    from_t = nt(parts_t, av_ref[...])
    from_s = nt(parts_s, au_ref[...])
    dfeat = (weight / den_tile) * cot_tile
    dfeat = dfeat + (from_t[0:32] + from_t[32:64] + from_t[64:96])
    dfeat = dfeat + (from_s[0:32] + from_s[32:64] + from_s[64:96])
    dfeat = dfeat * (1.0 / POS)
    back_ref[...] = (dfeat * gd_ref[...]).astype(BF16).astype(F32)
    grad_gd = jnp.sum(dfeat * act_ref[...], axis=0, keepdims=True)
    for r in range(8):
        small_ref[r : r + 1, :] = grad_gd[:, LANE * r : LANE * (r + 1)]
    for r in range(2):
        small_ref[8 + r : 9 + r, :] = grad_aw[:, LANE * r : LANE * (r + 1)]
    small_ref[10:16, :] = jnp.zeros((6, LANE), F32)


def backward_kernel(
    x_ref, mask_ref, hid_ref, up_ref, back_ref, small_ref, wd_ref, gu_ref,
    keep_ref, send_ref, extra_ref, down_acc, up_acc, gain_acc,
):
    step = pl.program_id(0)

    @pl.when(step == 0)
    def _():
        down_acc[...] = jnp.zeros_like(down_acc)
        up_acc[...] = jnp.zeros_like(up_acc)
        gain_acc[...] = jnp.zeros_like(gain_acc)

    rows = back_ref[pl.ds(pl.multiple_of(step * GROUP, GROUP), GROUP), :].astype(BF16)
    dback = jnp.concatenate(
        [
            mask_ref[POS * k : POS * (k + 1), :] * jnp.broadcast_to(rows[k : k + 1, :], (POS, FEAT))
            for k in range(GROUP)
        ],
        axis=0,
    )
    down_acc[...] += tn(hid_ref[...], dback)
    dhid = nt(dback, wd_ref[...])
    up = up_ref[...]
    gu = gu_ref[...]
    dscaled = jnp.where(up * gu > 0, dhid, 0.0)
    gain_acc[...] += jnp.sum((dscaled * up).reshape(ROWS // 8, 8, BOT), axis=0)
    dup = (dscaled * gu).astype(BF16)
    up_acc[...] += tn(dup, x_ref[...])

    @pl.when(step == STEPS - 1)
    def _():
        core = lax.axis_index("core")
        gain = jnp.sum(gain_acc[...], axis=0, keepdims=True)
        small = jnp.concatenate(
            [
                small_ref[0:10, :],
                gain[:, 0:LANE],
                gain[:, LANE : 2 * LANE],
                jnp.zeros((HALF - 12, LANE), F32),
            ],
            axis=0,
        )
        down = down_acc[...]
        up_grad = up_acc[...]
        send_ref[BOT : BOT + HALF, :] = jnp.zeros((HALF, FEAT), BF16)

        @pl.when(core == 0)
        def _():
            keep_ref[...] = down
            extra_ref[...] = small
            send_ref[0:BOT, :] = up_grad.astype(BF16)

        @pl.when(core != 0)
        def _():
            keep_ref[...] = up_grad
            extra_ref[...] = jnp.zeros((HALF, LANE), F32)
            send_ref[0:BOT, :] = down.astype(BF16)
            send_ref[BOT : BOT + HALF, 0:LANE] = small.astype(BF16)


def paired_kernel(keep_a_ref, got_a_ref, keep_b_ref, got_b_ref, extra_ref, out_ref):
    for p in range(N_PLANE):
        at = slice(HALF * p, HALF * (p + 1))
        for j in range(BLOCKS):
            lanes = slice(LANE * j, LANE * (j + 1))
            sum_a = keep_a_ref[at, lanes] + got_a_ref[at, lanes].astype(F32)
            sum_b = keep_b_ref[at, lanes] + got_b_ref[at, lanes].astype(F32)
            out_ref[p, PIECE * j : PIECE * j + HALF, :] = sum_a.astype(BF16)
            out_ref[p, PIECE * j + HALF : PIECE * (j + 1), :] = sum_b.astype(BF16)
        if p == 0:
            small = extra_ref[...] + got_b_ref[BOT : BOT + HALF, 0:LANE].astype(F32)
            out_ref[p, MAIN:TALL, :] = small.astype(BF16)
        else:
            out_ref[p, MAIN:TALL, :] = jnp.zeros((HALF, LANE), BF16)


def plane_sum_kernel(got_ref, out_ref):
    total = got_ref[0].astype(F32)
    for p in range(1, N_PLANE):
        total = total + got_ref[p].astype(F32)
    for j in range(N_Z):
        out_ref[j, 0:PIECE, :] = total[PIECE * j : PIECE * (j + 1)]
        out_ref[j, PIECE:, :] = total[MAIN:TALL]


def z_sum_kernel(got_ref, out_ref, small_ref):
    total = got_ref[0]
    for p in range(1, N_Z):
        total = total + got_ref[p]
    main = total[0:PIECE].astype(BF16)
    for j in range(N_Z):
        out_ref[j] = main
    small_ref[...] = total[PIECE:].astype(BF16)


def join_kernel(got_ref, small_ref, out_ref):
    for p in range(N_PLANE):
        for j in range(N_Z):
            out_ref[p, PIECE * j : PIECE * (j + 1), :] = got_ref[j]
        out_ref[p, MAIN:TALL, :] = small_ref[...]


def unpack_kernel(
    mine_ref, other_ref, sm_ref, so_ref,
    up_ref, down_ref, v_ref, u_ref, gup_ref, gdown_ref, aw_ref,
):
    first = lax.axis_index("core") == 0
    for j in range(2):
        attn = slice(PIECE * j, PIECE * j + HALF)
        enc = slice(PIECE * j + HALF, PIECE * (j + 1))
        lanes = slice(LANE * j, LANE * (j + 1))
        am = mine_ref[:, attn, :].astype(F32).reshape(ATT, LANE)
        ao = other_ref[:, attn, :].astype(F32).reshape(ATT, LANE)
        bm = mine_ref[:, enc, :].astype(F32).reshape(BOT, LANE)
        bo = other_ref[:, enc, :].astype(F32).reshape(BOT, LANE)
        v_ref[lanes, :] = jnp.where(first, am, ao).T
        u_ref[lanes, :] = jnp.where(first, ao, am).T
        down_ref[:, lanes] = jnp.where(first, bm, bo)
        up_ref[lanes, :] = jnp.where(first, bo, bm).T
    small = jnp.where(first, sm_ref[0].astype(F32), so_ref[0].astype(F32))
    for r in range(8):
        gdown_ref[:, LANE * r : LANE * (r + 1)] = small[r : r + 1, :]
    for r in range(2):
        aw_ref[:, LANE * r : LANE * (r + 1)] = small[8 + r : 9 + r, :]
        gup_ref[:, LANE * r : LANE * (r + 1)] = small[10 + r : 11 + r, :]


def whole_spec(shape):
    return pl.BlockSpec(shape, lambda *_: (0,) * len(shape))


def call(body, outs, *args, name):
    return pl.pallas_call(
        body,
        out_shape=[jax.ShapeDtypeStruct(s, d) for s, d in outs],
        compiler_params=params(),
        name=name,
    )(*args)


def swap(v):
    return lax.ppermute(v, "core", [(0, 1), (1, 0)])


def in_hbm(*arrays):
    return [pltpu.with_memory_space_constraint(v, pltpu.HBM) for v in arrays]


def reduce_all(keep_a, got_a, keep_b, got_b, extra):
    pieces = (N_PLANE, TALL, LANE)
    (paired,) = call(
        paired_kernel, [(pieces, BF16)], keep_a, got_a, keep_b, got_b, extra, name="paired"
    )
    got = lax.all_to_all(paired, PLANE, 0, 0, tiled=True)
    (parts,) = call(
        plane_sum_kernel, [((N_Z, PIECE + HALF, LANE), F32)], got, name="plane_sum"
    )
    got = lax.all_to_all(parts, "z", 0, 0, tiled=True)
    main, small = call(
        z_sum_kernel,
        [((N_Z, PIECE, LANE), BF16), ((HALF, LANE), BF16)],
        got,
        name="z_sum",
    )
    got = lax.all_to_all(main, "z", 0, 0, tiled=True)
    (whole,) = call(join_kernel, [(pieces, BF16)], got, small, name="join")
    return lax.all_to_all(whole, PLANE, 0, 0, tiled=True)


def per_device(
    tiles, counts, slide_ids, pooled_cot, w_up, w_down, gain_up, gain_down, attn_v, attn_u, attn_w
):
    rows = tiles.reshape(SLOTS * POS, FEAT)
    gu = gain_up.reshape(1, BOT)
    gd = gain_down.reshape(1, FEAT)
    aw = attn_w.reshape(1, ATT)
    smem = pl.BlockSpec(memory_space=pltpu.SMEM)
    mask, hid, up, feat, act, tanh, sigm, weight, pack = pl.pallas_call(
        forward_kernel,
        grid=(STEPS,),
        in_specs=[
            smem,
            pl.BlockSpec((ROWS, FEAT), lambda i: (i, 0)),
            whole_spec((1, SLOTS)),
            whole_spec((4, 32)),
            whole_spec((FEAT, BOT)),
            whole_spec((BOT, FEAT)),
            whole_spec((1, BOT)),
            whole_spec((1, FEAT)),
            whole_spec((FEAT, ATT)),
            whole_spec((FEAT, ATT)),
            whole_spec((1, ATT)),
        ],
        out_specs=[
            pl.BlockSpec((ROWS, FEAT), lambda i: (i, 0)),
            pl.BlockSpec((ROWS, BOT), lambda i: (i, 0)),
            pl.BlockSpec((ROWS, BOT), lambda i: (i, 0)),
            whole_spec((SLOTS, FEAT)),
            whole_spec((SLOTS, FEAT)),
            whole_spec((SLOTS, ATT)),
            whole_spec((SLOTS, ATT)),
            whole_spec((SLOTS, LANE)),
            whole_spec((40, LANE)),
        ],
        out_shape=[
            jax.ShapeDtypeStruct((SLOTS * POS, FEAT), BF16),
            jax.ShapeDtypeStruct((SLOTS * POS, BOT), BF16),
            jax.ShapeDtypeStruct((SLOTS * POS, BOT), F32),
            jax.ShapeDtypeStruct((SLOTS, FEAT), F32),
            jax.ShapeDtypeStruct((SLOTS, FEAT), F32),
            jax.ShapeDtypeStruct((SLOTS, ATT), F32),
            jax.ShapeDtypeStruct((SLOTS, ATT), F32),
            jax.ShapeDtypeStruct((SLOTS, LANE), F32),
            jax.ShapeDtypeStruct((40, LANE), F32),
        ],
        compiler_params=params(),
        name="encode",
    )(counts, *in_hbm(rows, slide_ids, pooled_cot, w_up, w_down, gu, gd, attn_v, attn_u, aw))

    (pairs,) = call(pair_kernel, [((N_PEERS, 24, LANE), F32)], pack, swap(pack), name="pair")
    got = lax.all_to_all(pairs, PEERS, 0, 0, tiled=True)
    other = swap(got)

    vmem = pl.BlockSpec(memory_space=pltpu.VMEM)
    back, pooled, small, keep_a, send_a = pl.pallas_call(
        middle_kernel,
        in_specs=[smem] + [vmem] * 12,
        out_shape=[
            jax.ShapeDtypeStruct((SLOTS, FEAT), F32),
            jax.ShapeDtypeStruct((4, FEAT), F32),
            jax.ShapeDtypeStruct((16, LANE), F32),
            jax.ShapeDtypeStruct((ATT, FEAT), F32),
            jax.ShapeDtypeStruct((ATT, FEAT), BF16),
        ],
        compiler_params=params(),
        name="middle",
    )(counts, slide_ids, got, other, feat, act, tanh, sigm, weight, attn_v, attn_u, aw, gd)

    got_a = swap(send_a)
    keep_b, send_b, extra = pl.pallas_call(
        backward_kernel,
        grid=(STEPS,),
        in_specs=[
            pl.BlockSpec((ROWS, FEAT), lambda i: (i, 0)),
            pl.BlockSpec((ROWS, FEAT), lambda i: (i, 0)),
            pl.BlockSpec((ROWS, BOT), lambda i: (i, 0)),
            pl.BlockSpec((ROWS, BOT), lambda i: (i, 0)),
            whole_spec((SLOTS, FEAT)),
            whole_spec((16, LANE)),
            whole_spec((BOT, FEAT)),
            whole_spec((1, BOT)),
        ],
        out_specs=[
            whole_spec((BOT, FEAT)),
            whole_spec((BOT + HALF, FEAT)),
            whole_spec((HALF, LANE)),
        ],
        out_shape=[
            jax.ShapeDtypeStruct((BOT, FEAT), F32),
            jax.ShapeDtypeStruct((BOT + HALF, FEAT), BF16),
            jax.ShapeDtypeStruct((HALF, LANE), F32),
        ],
        scratch_shapes=[
            pltpu.VMEM((BOT, FEAT), F32),
            pltpu.VMEM((BOT, FEAT), F32),
            pltpu.VMEM((8, BOT), F32),
        ],
        compiler_params=params(),
        name="backward",
    )(rows, mask, hid, up, back, small, w_down, gu)

    mine = reduce_all(keep_a, got_a, keep_b, swap(send_b), extra)
    other = swap(mine)

    part = pl.BlockSpec((N_PLANE, 2 * PIECE, LANE), lambda i: (0, i, 0))
    tail = pl.BlockSpec((1, HALF, LANE), lambda i: (0, MAIN // HALF, 0))
    wide = pl.BlockSpec((BOT, 2 * LANE), lambda i: (0, i))
    tall = pl.BlockSpec((2 * LANE, BOT), lambda i: (i, 0))
    g_up, g_down, g_v, g_u, g_gu, g_gd, g_aw = pl.pallas_call(
        unpack_kernel,
        grid=(4,),
        in_specs=[part, part, tail, tail],
        out_specs=[
            tall,
            wide,
            tall,
            tall,
            whole_spec((1, BOT)),
            whole_spec((1, FEAT)),
            whole_spec((1, ATT)),
        ],
        out_shape=[
            jax.ShapeDtypeStruct((FEAT, BOT), F32),
            jax.ShapeDtypeStruct((BOT, FEAT), F32),
            jax.ShapeDtypeStruct((FEAT, ATT), F32),
            jax.ShapeDtypeStruct((FEAT, ATT), F32),
            jax.ShapeDtypeStruct((1, BOT), F32),
            jax.ShapeDtypeStruct((1, FEAT), F32),
            jax.ShapeDtypeStruct((1, ATT), F32),
        ],
        compiler_params=params(),
        name="unpack",
    )(mine, other, mine, other)
    return (
        pooled,
        g_up,
        g_down,
        g_gu.reshape(BOT),
        g_gd.reshape(FEAT),
        g_v,
        g_u,
        g_aw.reshape(ATT),
    )


def solution(mesh):
    fine = Mesh(mesh.devices.reshape(2, 4, 2, 8, 2), FINE)
    return jax.shard_map(
        per_device,
        mesh=fine,
        in_specs=(
            P(SLIDE, TILE, None, None),
            P(SLIDE, TILE),
            P(SLIDE, TILE),
            P(SLIDE, TILE),
            P(),
            P(),
            P(),
            P(),
            P(),
            P(),
            P(),
        ),
        out_specs=(P(SLIDE, None), P(), P(), P(), P(), P(), P(), P()),
        check_vma=False,
    )
```

```python
import functools

import jax
import jax.numpy as jnp
from jax import lax
from jax.experimental import pallas as pl
from jax.experimental.pallas import tpu as pltpu
from jax.sharding import Mesh
from jax.sharding import PartitionSpec as P

F32 = jnp.float32
BF16 = jnp.bfloat16

FINE = ("x_lo", "y", "x_hi", "z", "core")
SLIDE = ("x_lo", "y")
TILE = ("x_hi", "z", "core")
PLANE = ("x_lo", "y", "x_hi")
N_PLANE = 16
N_Z = 8

SLOTS = 32
POS = 64
FEAT = 1024
BOT = 256
ATT = 256
LANE = 128
STEPS = 4
GROUP = SLOTS // STEPS
PIECE = 32
HALF = 16
BLOCKS = FEAT // LANE
MAIN = PIECE * BLOCKS
TALL = MAIN + HALF
ROWS = GROUP * POS

CHUNKS = 8
CHUNK = SLOTS * POS // CHUNKS
LOADS = (512, 1536)

VMEM_LIMIT = 24 * 1024 * 1024
VMEM = pl.BlockSpec(memory_space=pltpu.VMEM)


def params():
    return pltpu.CompilerParams(vmem_limit_bytes=VMEM_LIMIT)


def nn(a, b):
    return jnp.dot(a, b, preferred_element_type=F32)


def nt(a, b):
    return lax.dot_general(a, b, (((1,), (1,)), ((), ())), preferred_element_type=F32)


def tn(a, b):
    return lax.dot_general(a, b, (((0,), (0,)), ((), ())), preferred_element_type=F32)


def sigmoid(v):
    return 1.0 / (1.0 + jnp.exp(-v))


def column(row):
    n = row.shape[1]
    i = lax.broadcasted_iota(jnp.int32, (n, n), 0)
    j = lax.broadcasted_iota(jnp.int32, (n, n), 1)
    return jnp.sum(jnp.where(i == j, jnp.broadcast_to(row, (n, n)), 0), axis=1, keepdims=True)


def members(ids_ref):
    ids = column(ids_ref[...])
    return [ids == c for c in range(4)], ids >= 0


def split3(v):
    hi = v.astype(BF16)
    rest = v - hi.astype(F32)
    mid = rest.astype(BF16)
    low = (rest - mid.astype(F32)).astype(BF16)
    return [hi, mid, low]


def slopes(tanh, sigm, aw):
    return aw * sigm * (1.0 - tanh * tanh), aw * tanh * sigm * (1.0 - sigm)


def forward_kernel(
    x_hbm, wu_hbm, wd_hbm, gu_hbm, gd_hbm, av_hbm, au_hbm, aw_hbm, ids_hbm, cot_hbm,
    x_ref, hid_ref, up_ref, feat_ref, tanh_ref, sigm_ref, weight_ref, pack_ref,
    wu_ref, wd_ref, gu_ref, gd_ref, av_ref, au_ref, aw_ref, ids_ref, cot_ref, sems,
):
    starts = [sum(LOADS[:i]) for i in range(len(LOADS))]
    loads = []
    for i, start in enumerate(starts):
        at = pl.ds(start, LOADS[i])
        loads.append(pltpu.make_async_copy(x_hbm.at[at, :], x_ref.at[at, :], sems.at[i]))
    pairs = [
        (wu_hbm, wu_ref),
        (gu_hbm, gu_ref),
        (wd_hbm, wd_ref),
        (gd_hbm, gd_ref),
        (av_hbm, av_ref),
        (au_hbm, au_ref),
        (aw_hbm, aw_ref),
        (ids_hbm, ids_ref),
        (cot_hbm, cot_ref),
    ]
    others = [
        pltpu.make_async_copy(src, dst, sems.at[len(LOADS) + i])
        for i, (src, dst) in enumerate(pairs)
    ]
    others[0].start()
    loads[0].start()
    for copy in others[1:4]:
        copy.start()
    for copy in loads[1:]:
        copy.start()
    for copy in others[4:]:
        copy.start()
    for copy in others[:4]:
        copy.wait()
    for i in range(CHUNKS):
        at = slice(i * CHUNK, (i + 1) * CHUNK)
        if i * CHUNK in starts:
            loads[starts.index(i * CHUNK)].wait()
        x = x_ref[at, :]
        up = nn(x, wu_ref[...])
        up_ref[at, :] = up
        hidden = jnp.maximum(up * gu_ref[...], 0.0).astype(BF16)
        hid_ref[at, :] = hidden
        down = nn(hidden, wd_ref[...])
        res = x.astype(F32) + down * gd_ref[...]
        feats = jnp.sum(jnp.maximum(res, 0.0).reshape(CHUNK // POS, POS, FEAT), axis=1)
        feat_ref[i * CHUNK // POS : (i + 1) * CHUNK // POS, :] = feats * (1.0 / POS)
    for copy in others[4:]:
        copy.wait()
    feat = feat_ref[...]
    feat_b = feat.astype(BF16)
    tanh = jnp.tanh(nn(feat_b, av_ref[...]))
    sigm = sigmoid(nn(feat_b, au_ref[...]))
    tanh_ref[...] = tanh
    sigm_ref[...] = sigm
    weight = sigmoid(jnp.sum(tanh * sigm * aw_ref[...], axis=1, keepdims=True))
    weight_ref[...] = jnp.broadcast_to(weight, (SLOTS, LANE))
    member, _ = members(ids_ref)
    for c in range(4):
        share = jnp.where(member[c], weight, 0.0)
        num = jnp.sum(share * feat, axis=0, keepdims=True)
        den = jnp.sum(share, axis=0, keepdims=True)
        for r in range(8):
            pack_ref[8 * c + r : 8 * c + r + 1, :] = num[:, LANE * r : LANE * (r + 1)]
        pack_ref[36 + c : 37 + c, :] = jnp.broadcast_to(den, (1, LANE))
    quarter = lax.rem(lax.axis_index("z"), 2) * 2 + lax.axis_index("core")
    lane = lax.broadcasted_iota(jnp.int32, (4, LANE), 1)
    mine = jnp.logical_and(lane >= quarter * 32, lane < quarter * 32 + 32)
    cot = cot_ref[...].astype(F32)
    cot = jnp.concatenate([cot, cot, cot, cot], axis=1)
    pack_ref[32:36, :] = jnp.where(mine, cot, 0.0)


def keep_kernel(
    x_ref, hid_ref, wd_ref, gd_ref, tanh_ref, sigm_ref, aw_ref, av_ref, au_ref,
    mask_ref, act_ref, slope_ref,
):
    for i in range(CHUNKS):
        at = slice(i * CHUNK, (i + 1) * CHUNK)
        down = nn(hid_ref[at, :], wd_ref[...])
        positive = x_ref[at, :].astype(F32) + down * gd_ref[...] > 0
        mask_ref[at, :] = jnp.where(positive, 1.0, 0.0).astype(BF16)
        acts = jnp.where(positive, down, 0.0).reshape(CHUNK // POS, POS, FEAT)
        act_ref[i * CHUNK // POS : (i + 1) * CHUNK // POS, :] = jnp.sum(acts, axis=1)
    slope_t, slope_s = slopes(tanh_ref[...], sigm_ref[...], aw_ref[...])
    from_t = nt(jnp.concatenate(split3(slope_t), axis=0), av_ref[...])
    from_s = nt(jnp.concatenate(split3(slope_s), axis=0), au_ref[...])
    total = from_t[0:32] + from_t[32:64] + from_t[64:96]
    slope_ref[...] = total + (from_s[0:32] + from_s[32:64] + from_s[64:96])


def pair_kernel(mine_ref, other_ref, out_ref):
    out_ref[...] = mine_ref[...] + other_ref[...]


def spread_kernel(mine_ref, other_ref, out_ref):
    first = lax.axis_index("x_hi") == 0
    mine = mine_ref[...]
    other = other_ref[...]
    total = mine + other
    row = lax.broadcasted_iota(jnp.int32, (40, LANE), 0)
    cot = jnp.logical_and(row >= 32, row < 36)
    low = jnp.where(cot, jnp.where(first, mine, other), total)
    high = jnp.where(first, other, mine)[32:36]
    for p in range(N_Z):
        out_ref[p, 0:40, :] = low
        out_ref[p, 40:44, :] = high
        out_ref[p, 44:48, :] = high


def middle_kernel(
    ids_ref, got_ref, feat_ref, act_ref, slope_ref, tanh_ref, sigm_ref, weight_ref,
    aw_ref, gd_ref,
    back_ref, pooled_ref, small_ref, keep_ref, send_ref,
):
    core = lax.axis_index("core")
    total = got_ref[0]
    for p in range(1, N_Z):
        total = total + got_ref[p]
    cot = jnp.concatenate(
        [
            got_ref[2 * b, row : row + 4, :] + got_ref[2 * b + 1, row : row + 4, :]
            for row in (32, 40)
            for b in range(N_Z // 2)
        ],
        axis=1,
    )
    member, live = members(ids_ref)
    cot_tile = jnp.zeros((SLOTS, FEAT), F32)
    pooled_tile = jnp.zeros((SLOTS, FEAT), F32)
    den_tile = jnp.where(live, 0.0, 1.0)
    for c in range(4):
        num = jnp.concatenate([total[8 * c + r : 8 * c + r + 1, :] for r in range(8)], axis=1)
        den = total[36 + c : 37 + c, 0:1]
        pooled = num / den
        pooled_ref[c : c + 1, :] = pooled
        cot_tile = jnp.where(member[c], cot[c : c + 1, :], cot_tile)
        pooled_tile = jnp.where(member[c], pooled, pooled_tile)
        den_tile = jnp.where(member[c], den, den_tile)
    feat = feat_ref[...]
    tanh = tanh_ref[...]
    sigm = sigm_ref[...]
    weight = weight_ref[:, 0:1]
    aw = aw_ref[...]
    dweight = jnp.sum(cot_tile * (feat - pooled_tile), axis=1, keepdims=True) / den_tile
    dscore = dweight * weight * (1.0 - weight)
    grad_aw = jnp.sum(dscore * tanh * sigm, axis=0, keepdims=True)
    slope_t, slope_s = slopes(tanh, sigm, aw)
    parts_t = jnp.concatenate(split3(dscore * slope_t), axis=0)
    parts_s = jnp.concatenate(split3(dscore * slope_s), axis=0)
    feat_b = feat.astype(BF16)
    feat_3 = jnp.concatenate([feat_b, feat_b, feat_b], axis=0)
    grad_v = tn(parts_t, feat_3)
    grad_u = tn(parts_s, feat_3)

    @pl.when(core == 0)
    def _():
        keep_ref[...] = grad_v
        send_ref[...] = grad_u.astype(BF16)

    @pl.when(core != 0)
    def _():
        keep_ref[...] = grad_u
        send_ref[...] = grad_v.astype(BF16)

    dfeat = ((weight / den_tile) * cot_tile + dscore * slope_ref[...]) * (1.0 / POS)
    back_ref[...] = (dfeat * gd_ref[...]).astype(BF16).astype(F32)
    grad_gd = jnp.sum(dfeat * act_ref[...], axis=0, keepdims=True)
    for r in range(8):
        small_ref[r : r + 1, :] = grad_gd[:, LANE * r : LANE * (r + 1)]
    for r in range(2):
        small_ref[8 + r : 9 + r, :] = grad_aw[:, LANE * r : LANE * (r + 1)]
    small_ref[10:16, :] = jnp.zeros((6, LANE), F32)


def backward_kernel(
    x_ref, mask_ref, hid_ref, up_ref, back_ref, small_ref, wd_ref, gu_ref,
    keep_ref, send_ref, extra_ref, dback_ref, dup_ref,
):
    gu = gu_ref[...]
    gain = jnp.zeros((8, BOT), F32)
    for i in range(STEPS):
        at = slice(ROWS * i, ROWS * (i + 1))
        for k in range(GROUP):
            tile = GROUP * i + k
            row = back_ref[tile : tile + 1, :].astype(BF16)
            here = slice(POS * tile, POS * (tile + 1))
            dback_ref[here, :] = mask_ref[here, :] * jnp.broadcast_to(row, (POS, FEAT))
        dhid = nt(dback_ref[at, :], wd_ref[...])
        up = up_ref[at, :]
        dscaled = jnp.where(up * gu > 0, dhid, 0.0)
        gain = gain + jnp.sum((dscaled * up).reshape(ROWS // 8, 8, BOT), axis=0)
        dup_ref[at, :] = (dscaled * gu).astype(BF16)
    gain = jnp.sum(gain, axis=0, keepdims=True)
    small = jnp.concatenate(
        [
            small_ref[0:10, :],
            gain[:, 0:LANE],
            gain[:, LANE : 2 * LANE],
            jnp.zeros((HALF - 12, LANE), F32),
        ],
        axis=0,
    )
    first = lax.axis_index("core") == 0
    down = tn(hid_ref[...], dback_ref[...])
    up_grad = tn(dup_ref[...], x_ref[...])

    @pl.when(first)
    def _():
        keep_ref[...] = down
        extra_ref[...] = small
        send_ref[0:BOT, :] = up_grad.astype(BF16)

    @pl.when(jnp.logical_not(first))
    def _():
        keep_ref[...] = up_grad
        extra_ref[...] = jnp.zeros((HALF, LANE), F32)
        send_ref[0:BOT, :] = down.astype(BF16)

    sent = jnp.where(first, 0.0, small)
    high = sent.astype(BF16)
    send_ref[BOT : BOT + HALF, :] = jnp.zeros((HALF, FEAT), BF16)
    send_ref[BOT : BOT + HALF, 0:LANE] = high
    send_ref[BOT : BOT + HALF, LANE : 2 * LANE] = (sent - high.astype(F32)).astype(BF16)


def two_terms(row):
    high = row.astype(BF16).astype(F32)
    rows = lax.broadcasted_iota(jnp.int32, (HALF, LANE), 0)
    block = jnp.where(rows == 0, high, jnp.where(rows == 1, row - high, 0.0))
    return block.astype(BF16)


def paired_kernel(keep_a_ref, got_a_ref, keep_b_ref, got_b_ref, extra_ref, out_ref):
    for p in range(N_PLANE):
        at = slice(HALF * p, HALF * (p + 1))
        for j in range(BLOCKS):
            lanes = slice(LANE * j, LANE * (j + 1))
            sum_a = keep_a_ref[at, lanes] + got_a_ref[at, lanes].astype(F32)
            sum_b = keep_b_ref[at, lanes] + got_b_ref[at, lanes].astype(F32)
            out_ref[p, PIECE * j : PIECE * j + HALF, :] = sum_a.astype(BF16)
            out_ref[p, PIECE * j + HALF : PIECE * (j + 1), :] = sum_b.astype(BF16)
        cols = slice(0, LANE), slice(LANE, 2 * LANE)
        small = extra_ref[p : p + 1, :]
        for col in cols:
            small = small + got_b_ref[BOT : BOT + HALF, col].astype(F32)[p : p + 1, :]
        out_ref[p, MAIN:TALL, :] = two_terms(small)


def small_row(block):
    return block[MAIN : MAIN + 1, :].astype(F32) + block[MAIN + 1 : MAIN + 2, :].astype(F32)


def plane_sum_kernel(got_ref, out_ref):
    total = got_ref[0].astype(F32)
    for p in range(1, N_PLANE):
        total = total + got_ref[p].astype(F32)
    out_ref[0:MAIN, :] = total[0:MAIN].astype(BF16)
    out_ref[MAIN:TALL, :] = two_terms(small_row(total))


def z_pair_kernel(mine_ref, other_ref, out_ref):
    total = mine_ref[0:MAIN, :].astype(F32) + other_ref[0:MAIN, :].astype(F32)
    out_ref[0:MAIN, :] = total.astype(BF16)
    out_ref[MAIN:TALL, :] = two_terms(small_row(mine_ref) + small_row(other_ref))


def z_sum_kernel(mine_ref, near_ref, far_ref, cross_ref, out_ref):
    near = mine_ref[0:MAIN, :].astype(F32) + near_ref[0:MAIN, :].astype(F32)
    far = far_ref[0:MAIN, :].astype(F32) + cross_ref[0:MAIN, :].astype(F32)
    main = (near + far).astype(BF16)
    near = small_row(mine_ref) + small_row(near_ref)
    far = small_row(far_ref) + small_row(cross_ref)
    small = two_terms(near + far)
    for p in range(N_PLANE):
        out_ref[p, 0:MAIN, :] = main
        out_ref[p, MAIN:TALL, :] = small


def unpack_kernel(own, got_ref, *refs):
    up_hbm, down_hbm, v_hbm, u_hbm, gup_hbm, gdown_hbm, aw_hbm = refs[-14:-7]
    attn_ref, down_ref, up_ref, gup_ref, gdown_ref, aw_ref, sems = refs[-7:]
    first = (lax.axis_index("core") == 0) if own else (lax.axis_index("core") != 0)
    to_v = pltpu.make_async_copy(attn_ref, v_hbm, sems.at[0])
    to_u = pltpu.make_async_copy(attn_ref, u_hbm, sems.at[0])
    to_down = pltpu.make_async_copy(down_ref, down_hbm, sems.at[1])
    to_up = pltpu.make_async_copy(up_ref, up_hbm, sems.at[1])
    smalls = [
        pltpu.make_async_copy(gup_ref, gup_hbm, sems.at[2]),
        pltpu.make_async_copy(gdown_ref, gdown_hbm, sems.at[3]),
        pltpu.make_async_copy(aw_ref, aw_hbm, sems.at[4]),
    ]
    for j in range(BLOCKS):
        rows = slice(PIECE * j, PIECE * j + HALF)
        attn = got_ref[:, rows, :].astype(F32).reshape(ATT, LANE)
        attn_ref[LANE * j : LANE * (j + 1), :] = attn.T

    @pl.when(first)
    def _():
        to_v.start()
        for j in range(BLOCKS):
            rows = slice(PIECE * j + HALF, PIECE * (j + 1))
            enc = got_ref[:, rows, :].astype(F32).reshape(BOT, LANE)
            down_ref[:, LANE * j : LANE * (j + 1)] = enc
        to_down.start()
        for r in range(12):
            block = got_ref[r, MAIN:TALL, :].astype(F32)
            small = block[0:1, :] + block[1:2, :]
            if r < 8:
                gdown_ref[:, LANE * r : LANE * (r + 1)] = small
            elif r < 10:
                aw_ref[:, LANE * (r - 8) : LANE * (r - 7)] = small
            else:
                gup_ref[:, LANE * (r - 10) : LANE * (r - 9)] = small
        for copy in smalls:
            copy.start()
        to_v.wait()
        to_down.wait()
        for copy in smalls:
            copy.wait()

    @pl.when(jnp.logical_not(first))
    def _():
        to_u.start()
        for j in range(BLOCKS):
            rows = slice(PIECE * j + HALF, PIECE * (j + 1))
            enc = got_ref[:, rows, :].astype(F32).reshape(BOT, LANE)
            up_ref[LANE * j : LANE * (j + 1), :] = enc.T
        to_up.start()
        to_u.wait()
        to_up.wait()


def whole_spec(shape):
    return pl.BlockSpec(shape, lambda *_: (0,) * len(shape))


def call(body, outs, *args, name):
    return pl.pallas_call(
        body,
        out_shape=[jax.ShapeDtypeStruct(s, d) for s, d in outs],
        compiler_params=params(),
        name=name,
    )(*args)


def swap(v, axis):
    return lax.ppermute(v, axis, [(0, 1), (1, 0)])


def in_hbm(*arrays):
    return [pltpu.with_memory_space_constraint(v, pltpu.HBM) for v in arrays]


def reduce_all(keep_a, got_a, keep_b, got_b, extra):
    pieces = (N_PLANE, TALL, LANE)
    (paired,) = call(
        paired_kernel, [(pieces, BF16)], keep_a, got_a, keep_b, got_b, extra, name="paired"
    )
    got = lax.all_to_all(paired, PLANE, 0, 0, tiled=True)
    flat = [(pieces[1:], BF16)]
    (part,) = call(plane_sum_kernel, flat, got, name="plane_sum")
    (pair,) = call(z_pair_kernel, flat, part, cross_z(part, 1), name="z_pair")
    (whole,) = call(
        z_sum_kernel,
        [(pieces, BF16)],
        pair, cross_z(pair, 2), cross_z(pair, 4), cross_z(pair, 6),
        name="z_sum",
    )
    return lax.all_to_all(whole, PLANE, 0, 0, tiled=True)


def cross_z(v, bits):
    return lax.ppermute(v, "z", [(i, i ^ bits) for i in range(N_Z)])


def unpack(got, *before):
    hbm = pl.BlockSpec(memory_space=pltpu.HBM)
    shapes = [
        (FEAT, BOT), (BOT, FEAT), (FEAT, ATT), (FEAT, ATT), (1, BOT), (1, FEAT), (1, ATT)
    ]
    return pl.pallas_call(
        functools.partial(unpack_kernel, not before),
        in_specs=[VMEM] + [hbm] * len(before),
        out_specs=[hbm] * len(shapes),
        out_shape=[jax.ShapeDtypeStruct(v, F32) for v in shapes],
        input_output_aliases={1 + i: i for i in range(len(before))},
        scratch_shapes=[
            pltpu.VMEM((FEAT, ATT), F32),
            pltpu.VMEM((BOT, FEAT), F32),
            pltpu.VMEM((FEAT, BOT), F32),
            pltpu.VMEM((1, BOT), F32),
            pltpu.VMEM((1, FEAT), F32),
            pltpu.VMEM((1, ATT), F32),
            pltpu.SemaphoreType.DMA((5,)),
        ],
        compiler_params=params(),
        name="unpack_other" if before else "unpack_own",
    )(got, *before)


def encode(
    rows, ids, pooled_cot, w_up, w_down, gu, gd, attn_v, attn_u, aw
):
    hbm = pl.BlockSpec(memory_space=pltpu.HBM)
    outs = [
        ((SLOTS * POS, FEAT), BF16),
        ((SLOTS * POS, BOT), BF16),
        ((SLOTS * POS, BOT), F32),
        ((SLOTS, FEAT), F32),
        ((SLOTS, ATT), F32),
        ((SLOTS, ATT), F32),
        ((SLOTS, LANE), F32),
        ((40, LANE), F32),
    ]
    return pl.pallas_call(
        forward_kernel,
        in_specs=[hbm] * 10,
        out_specs=[VMEM] * len(outs),
        out_shape=[jax.ShapeDtypeStruct(s, d) for s, d in outs],
        scratch_shapes=[
            pltpu.VMEM((FEAT, BOT), BF16),
            pltpu.VMEM((BOT, FEAT), BF16),
            pltpu.VMEM((1, BOT), F32),
            pltpu.VMEM((1, FEAT), F32),
            pltpu.VMEM((FEAT, ATT), BF16),
            pltpu.VMEM((FEAT, ATT), BF16),
            pltpu.VMEM((1, ATT), F32),
            pltpu.VMEM((1, SLOTS), jnp.int32),
            pltpu.VMEM((4, 32), BF16),
            pltpu.SemaphoreType.DMA((len(LOADS) + 9,)),
        ],
        compiler_params=params(),
        name="encode",
    )(*in_hbm(rows, w_up, w_down, gu, gd, attn_v, attn_u, aw, ids, pooled_cot))


def backward(x, mask, hid, up, back, small, w_down, gu):
    return pl.pallas_call(
        backward_kernel,
        in_specs=[VMEM] * 8,
        out_shape=[
            jax.ShapeDtypeStruct((BOT, FEAT), F32),
            jax.ShapeDtypeStruct((BOT + HALF, FEAT), BF16),
            jax.ShapeDtypeStruct((HALF, LANE), F32),
        ],
        scratch_shapes=[
            pltpu.VMEM((SLOTS * POS, FEAT), BF16),
            pltpu.VMEM((SLOTS * POS, BOT), BF16),
        ],
        compiler_params=params(),
        name="backward",
    )(x, mask, hid, up, back, small, w_down, gu)


def per_device(
    tiles, counts, slide_ids, pooled_cot, w_up, w_down, gain_up, gain_down, attn_v, attn_u, attn_w
):
    rows = tiles.reshape(SLOTS * POS, FEAT)
    gu = gain_up.reshape(1, BOT)
    gd = gain_down.reshape(1, FEAT)
    aw = attn_w.reshape(1, ATT)
    slot = lax.broadcasted_iota(jnp.int32, (1, SLOTS), 1)
    ids = jnp.where(slot < counts, slide_ids, -1)
    x, hid, up, feat, tanh, sigm, weight, pack = encode(
        rows, ids, pooled_cot, w_up, w_down, gu, gd, attn_v, attn_u, aw
    )
    (half,) = call(pair_kernel, [((40, LANE), F32)], pack, swap(pack, "core"), name="pair")
    mask, act, slope = call(
        keep_kernel,
        [((SLOTS * POS, FEAT), BF16), ((SLOTS, FEAT), F32), ((SLOTS, FEAT), F32)],
        x, hid, w_down, gd, tanh, sigm, aw, attn_v, attn_u,
        name="keep",
    )
    across, mask, act, slope = lax.optimization_barrier((swap(half, "x_hi"), mask, act, slope))
    (spread,) = call(spread_kernel, [((N_Z, 48, LANE), F32)], half, across, name="spread")
    got = lax.all_to_all(spread, "z", 0, 0, tiled=True)

    back, pooled, small, keep_a, send_a = pl.pallas_call(
        middle_kernel,
        in_specs=[VMEM] * 10,
        out_shape=[
            jax.ShapeDtypeStruct((SLOTS, FEAT), F32),
            jax.ShapeDtypeStruct((4, FEAT), F32),
            jax.ShapeDtypeStruct((16, LANE), F32),
            jax.ShapeDtypeStruct((ATT, FEAT), F32),
            jax.ShapeDtypeStruct((ATT, FEAT), BF16),
        ],
        compiler_params=params(),
        name="middle",
    )(ids, got, feat, act, slope, tanh, sigm, weight, aw, gd)

    got_a = swap(send_a, "core")
    keep_b, send_b, extra = backward(x, mask, hid, up, back, small, w_down, gu)
    got_b = swap(send_b, "core")

    mine = reduce_all(keep_a, got_a, keep_b, got_b, extra)
    other = swap(mine, "core")
    g_up, g_down, g_v, g_u, g_gu, g_gd, g_aw = unpack(other, *unpack(mine))
    return (
        pooled,
        g_up,
        g_down,
        g_gu.reshape(BOT),
        g_gd.reshape(FEAT),
        g_v,
        g_u,
        g_aw.reshape(ATT),
    )


def solution(mesh):
    fine = Mesh(mesh.devices.reshape(2, 4, 2, 8, 2), FINE)
    return jax.shard_map(
        per_device,
        mesh=fine,
        in_specs=(
            P(SLIDE, TILE, None, None),
            P(SLIDE, TILE),
            P(SLIDE, TILE),
            P(SLIDE, TILE),
            P(),
            P(),
            P(),
            P(),
            P(),
            P(),
            P(),
        ),
        out_specs=(P(SLIDE, None), P(), P(), P(), P(), P(), P(), P()),
        check_vma=False,
    )
```

```python
import functools

import jax
import jax.numpy as jnp
from jax import lax
from jax.experimental import pallas as pl
from jax.experimental.pallas import tpu as pltpu
from jax.sharding import Mesh
from jax.sharding import PartitionSpec as P

F32 = jnp.float32
BF16 = jnp.bfloat16

FINE = ("x_lo", "y", "x_hi", "z", "core")
SLIDE = ("x_lo", "y")
TILE = ("x_hi", "z", "core")
PLANE = ("x_lo", "y", "x_hi")
N_PLANE = 16
N_Z = 8

SLOTS = 32
POS = 64
FEAT = 1024
BOT = 256
ATT = 256
LANE = 128
STEPS = 4
GROUP = SLOTS // STEPS
PIECE = 32
HALF = 16
BLOCKS = FEAT // LANE
MAIN = PIECE * BLOCKS
TALL = MAIN + HALF
ROWS = GROUP * POS

CHUNKS = 8
CHUNK = SLOTS * POS // CHUNKS
LOADS = (512, 1536)

VMEM_LIMIT = 24 * 1024 * 1024
VMEM = pl.BlockSpec(memory_space=pltpu.VMEM)


def params():
    return pltpu.CompilerParams(vmem_limit_bytes=VMEM_LIMIT)


def nn(a, b):
    return jnp.dot(a, b, preferred_element_type=F32)


def nt(a, b):
    return lax.dot_general(a, b, (((1,), (1,)), ((), ())), preferred_element_type=F32)


def tn(a, b):
    return lax.dot_general(a, b, (((0,), (0,)), ((), ())), preferred_element_type=F32)


def sigmoid(v):
    return 1.0 / (1.0 + jnp.exp(-v))


def column(row):
    n = row.shape[1]
    i = lax.broadcasted_iota(jnp.int32, (n, n), 0)
    j = lax.broadcasted_iota(jnp.int32, (n, n), 1)
    return jnp.sum(jnp.where(i == j, jnp.broadcast_to(row, (n, n)), 0), axis=1, keepdims=True)


def members(ids_ref):
    ids = column(ids_ref[...])
    return [ids == c for c in range(4)], ids >= 0


def split3(v):
    hi = v.astype(BF16)
    rest = v - hi.astype(F32)
    mid = rest.astype(BF16)
    low = (rest - mid.astype(F32)).astype(BF16)
    return [hi, mid, low]


def slopes(tanh, sigm, aw):
    return aw * sigm * (1.0 - tanh * tanh), aw * tanh * sigm * (1.0 - sigm)


def forward_kernel(
    x_hbm, wu_hbm, wd_hbm, gu_hbm, gd_hbm, av_hbm, au_hbm, aw_hbm, ids_hbm, cot_hbm, count_ref,
    x_ref, hid_ref, up_ref, feat_ref, tanh_ref, sigm_ref, weight_ref, pack_ref, live_ref,
    wd_ref, gu_ref, gd_ref, av_ref, au_ref, aw_ref, wu_ref, ids_ref, cot_ref, sems,
):
    starts = [sum(LOADS[:i]) for i in range(len(LOADS))]
    loads = []
    for i, start in enumerate(starts):
        at = pl.ds(start, LOADS[i])
        loads.append(pltpu.make_async_copy(x_hbm.at[at, :], x_ref.at[at, :], sems.at[i]))
    pairs = [
        (wu_hbm, wu_ref),
        (gu_hbm, gu_ref),
        (wd_hbm, wd_ref),
        (gd_hbm, gd_ref),
        (av_hbm, av_ref),
        (au_hbm, au_ref),
        (aw_hbm, aw_ref),
        (ids_hbm, ids_ref),
        (cot_hbm, cot_ref),
    ]
    others = [
        pltpu.make_async_copy(src, dst, sems.at[len(LOADS) + i])
        for i, (src, dst) in enumerate(pairs)
    ]
    others[0].start()
    loads[0].start()
    for copy in others[1:4]:
        copy.start()
    for copy in loads[1:]:
        copy.start()
    for copy in others[4:]:
        copy.start()
    for copy in others[:4]:
        copy.wait()
    for i in range(CHUNKS):
        at = slice(i * CHUNK, (i + 1) * CHUNK)
        if i * CHUNK in starts:
            loads[starts.index(i * CHUNK)].wait()
        x = x_ref[at, :]
        up = nn(x, wu_ref[...])
        up_ref[at, :] = up
        hidden = jnp.maximum(up * gu_ref[...], 0.0).astype(BF16)
        hid_ref[at, :] = hidden
        down = nn(hidden, wd_ref[...])
        res = x.astype(F32) + down * gd_ref[...]
        feats = jnp.sum(jnp.maximum(res, 0.0).reshape(CHUNK // POS, POS, FEAT), axis=1)
        feat_ref[i * CHUNK // POS : (i + 1) * CHUNK // POS, :] = feats * (1.0 / POS)
    for copy in others[4:]:
        copy.wait()
    feat = feat_ref[...]
    feat_b = feat.astype(BF16)
    tanh = jnp.tanh(nn(feat_b, av_ref[...]))
    sigm = sigmoid(nn(feat_b, au_ref[...]))
    tanh_ref[...] = tanh
    sigm_ref[...] = sigm
    weight = sigmoid(jnp.sum(tanh * sigm * aw_ref[...], axis=1, keepdims=True))
    weight_ref[...] = jnp.broadcast_to(weight, (SLOTS, LANE))
    slot = lax.broadcasted_iota(jnp.int32, (1, SLOTS), 1)
    live_ref[...] = jnp.where(slot < count_ref[0, 0], ids_ref[...], -1)
    member, _ = members(live_ref)
    for c in range(4):
        share = jnp.where(member[c], weight, 0.0)
        num = jnp.sum(share * feat, axis=0, keepdims=True)
        den = jnp.sum(share, axis=0, keepdims=True)
        for r in range(8):
            pack_ref[8 * c + r : 8 * c + r + 1, :] = num[:, LANE * r : LANE * (r + 1)]
        pack_ref[36 + c : 37 + c, :] = jnp.broadcast_to(den, (1, LANE))
    quarter = lax.rem(lax.axis_index("z"), 2) * 2 + lax.axis_index("core")
    lane = lax.broadcasted_iota(jnp.int32, (4, LANE), 1)
    mine = jnp.logical_and(lane >= quarter * 32, lane < quarter * 32 + 32)
    cot = cot_ref[...].astype(F32)
    cot = jnp.concatenate([cot, cot, cot, cot], axis=1)
    pack_ref[32:36, :] = jnp.where(mine, cot, 0.0)


def keep_kernel(
    x_ref, hid_ref, wd_ref, gd_ref, tanh_ref, sigm_ref, aw_ref, av_ref, au_ref,
    mask_ref, act_ref, slope_ref,
):
    for i in range(CHUNKS):
        at = slice(i * CHUNK, (i + 1) * CHUNK)
        down = nn(hid_ref[at, :], wd_ref[...])
        positive = x_ref[at, :].astype(F32) + down * gd_ref[...] > 0
        mask_ref[at, :] = jnp.where(positive, 1.0, 0.0).astype(BF16)
        acts = jnp.where(positive, down, 0.0).reshape(CHUNK // POS, POS, FEAT)
        act_ref[i * CHUNK // POS : (i + 1) * CHUNK // POS, :] = jnp.sum(acts, axis=1)
    slope_t, slope_s = slopes(tanh_ref[...], sigm_ref[...], aw_ref[...])
    from_t = nt(jnp.concatenate(split3(slope_t), axis=0), av_ref[...])
    from_s = nt(jnp.concatenate(split3(slope_s), axis=0), au_ref[...])
    total = from_t[0:32] + from_t[32:64] + from_t[64:96]
    slope_ref[...] = total + (from_s[0:32] + from_s[32:64] + from_s[64:96])


def pair_kernel(mine_ref, other_ref, out_ref):
    out_ref[...] = mine_ref[...] + other_ref[...]


def spread_kernel(mine_ref, other_ref, out_ref):
    first = lax.axis_index("x_hi") == 0
    mine = mine_ref[...]
    other = other_ref[...]
    total = mine + other
    row = lax.broadcasted_iota(jnp.int32, (40, LANE), 0)
    cot = jnp.logical_and(row >= 32, row < 36)
    low = jnp.where(cot, jnp.where(first, mine, other), total)
    high = jnp.where(first, other, mine)[32:36]
    for p in range(N_Z):
        out_ref[p, 0:40, :] = low
        out_ref[p, 40:44, :] = high
        out_ref[p, 44:48, :] = high


def middle_kernel(
    ids_ref, got_ref, feat_ref, act_ref, slope_ref, tanh_ref, sigm_ref, weight_ref,
    aw_ref, gd_ref,
    back_ref, pooled_ref, small_ref, keep_ref, send_ref, keep_sum_ref, profile_ref,
):
    core = lax.axis_index("core")
    total = got_ref[0]
    for p in range(1, N_Z):
        total = total + got_ref[p]
    cot = jnp.concatenate(
        [
            got_ref[2 * b, row : row + 4, :] + got_ref[2 * b + 1, row : row + 4, :]
            for row in (32, 40)
            for b in range(N_Z // 2)
        ],
        axis=1,
    )
    member, live = members(ids_ref)
    cot_tile = jnp.zeros((SLOTS, FEAT), F32)
    pooled_tile = jnp.zeros((SLOTS, FEAT), F32)
    den_tile = jnp.where(live, 0.0, 1.0)
    profile = jnp.zeros((1, FEAT), F32)
    for c in range(4):
        num = jnp.concatenate([total[8 * c + r : 8 * c + r + 1, :] for r in range(8)], axis=1)
        den = total[36 + c : 37 + c, 0:1]
        pooled = num / den
        pooled_ref[c : c + 1, :] = pooled
        profile = profile + pooled
        cot_tile = jnp.where(member[c], cot[c : c + 1, :], cot_tile)
        pooled_tile = jnp.where(member[c], pooled, pooled_tile)
        den_tile = jnp.where(member[c], den, den_tile)
    feat = feat_ref[...]
    tanh = tanh_ref[...]
    sigm = sigm_ref[...]
    weight = weight_ref[:, 0:1]
    aw = aw_ref[...]
    dweight = jnp.sum(cot_tile * (feat - pooled_tile), axis=1, keepdims=True) / den_tile
    dscore = dweight * weight * (1.0 - weight)
    grad_aw = jnp.sum(dscore * tanh * sigm, axis=0, keepdims=True)
    slope_t, slope_s = slopes(tanh, sigm, aw)
    grad_t = dscore * slope_t
    grad_s = dscore * slope_s
    profile = (profile * 0.25).astype(BF16).astype(F32)
    norm = jnp.maximum(jnp.sum(profile * profile, axis=1, keepdims=True), 1e-30)
    feat_b = feat.astype(BF16).astype(F32)
    along = jnp.sum(feat_b * profile, axis=1, keepdims=True) / norm
    rest = feat_b - along * profile
    rest_0, rest_1, _ = split3(rest)
    rest_3 = jnp.concatenate([rest_0, rest_0, rest_1], axis=0)
    grad_t0, grad_t1, _ = split3(grad_t)
    grad_s0, grad_s1, _ = split3(grad_s)
    grad_v = tn(jnp.concatenate([grad_t0, grad_t1, grad_t0], axis=0), rest_3)
    grad_u = tn(jnp.concatenate([grad_s0, grad_s1, grad_s0], axis=0), rest_3)
    sum_t = jnp.sum(along * grad_t, axis=0, keepdims=True)
    sum_s = jnp.sum(along * grad_s, axis=0, keepdims=True)
    for r in range(8):
        profile_ref[r : r + 1, :] = profile[:, LANE * r : LANE * (r + 1)]
    keep_sum_ref[...] = jnp.where(core == 0, sum_t, sum_s)
    sent = jnp.where(core == 0, sum_s, sum_t)
    high = sent.astype(BF16)
    send_ref[ATT : ATT + HALF, :] = jnp.zeros((HALF, FEAT), BF16)
    send_ref[ATT : ATT + HALF, 0:ATT] = jnp.broadcast_to(high, (HALF, ATT))
    low = (sent - high.astype(F32)).astype(BF16)
    send_ref[ATT : ATT + HALF, ATT : 2 * ATT] = jnp.broadcast_to(low, (HALF, ATT))

    @pl.when(core == 0)
    def _():
        keep_ref[...] = grad_v
        send_ref[0:ATT, :] = grad_u.astype(BF16)

    @pl.when(core != 0)
    def _():
        keep_ref[...] = grad_u
        send_ref[0:ATT, :] = grad_v.astype(BF16)

    dfeat = ((weight / den_tile) * cot_tile + dscore * slope_ref[...]) * (1.0 / POS)
    back_ref[...] = (dfeat * gd_ref[...]).astype(BF16).astype(F32)
    grad_gd = jnp.sum(dfeat * act_ref[...], axis=0, keepdims=True)
    for r in range(8):
        small_ref[r : r + 1, :] = grad_gd[:, LANE * r : LANE * (r + 1)]
    for r in range(2):
        small_ref[8 + r : 9 + r, :] = grad_aw[:, LANE * r : LANE * (r + 1)]
    small_ref[10:16, :] = jnp.zeros((6, LANE), F32)


def rows_kernel(
    mask_ref, up_ref, back_ref, small_ref, wd_ref, gu_ref, dback_ref, dup_ref, out_ref
):
    gu = gu_ref[...]
    gain = jnp.zeros((8, BOT), F32)
    for i in range(STEPS):
        at = slice(ROWS * i, ROWS * (i + 1))
        for k in range(GROUP):
            tile = GROUP * i + k
            row = back_ref[tile : tile + 1, :].astype(BF16)
            here = slice(POS * tile, POS * (tile + 1))
            dback_ref[here, :] = mask_ref[here, :] * jnp.broadcast_to(row, (POS, FEAT))
        dhid = nt(dback_ref[at, :], wd_ref[...])
        up = up_ref[at, :]
        dscaled = jnp.where(up * gu > 0, dhid, 0.0)
        gain = gain + jnp.sum((dscaled * up).reshape(ROWS // 8, 8, BOT), axis=0)
        dup_ref[at, :] = (dscaled * gu).astype(BF16)
    gain = jnp.sum(gain, axis=0, keepdims=True)
    out_ref[0:10, :] = small_ref[0:10, :]
    out_ref[10:11, :] = gain[:, 0:LANE]
    out_ref[11:12, :] = gain[:, LANE : 2 * LANE]
    out_ref[12:HALF, :] = jnp.zeros((HALF - 12, LANE), F32)


def sums_kernel(x_ref, hid_ref, dback_ref, dup_ref, small_ref, keep_ref, send_ref, extra_ref):
    small = small_ref[...]
    first = lax.axis_index("core") == 0
    down = tn(hid_ref[...], dback_ref[...])
    up_grad = tn(dup_ref[...], x_ref[...])

    @pl.when(first)
    def _():
        keep_ref[...] = down
        extra_ref[...] = small
        send_ref[0:BOT, :] = up_grad.astype(BF16)

    @pl.when(jnp.logical_not(first))
    def _():
        keep_ref[...] = up_grad
        extra_ref[...] = jnp.zeros((HALF, LANE), F32)
        send_ref[0:BOT, :] = down.astype(BF16)

    sent = jnp.where(first, 0.0, small)
    high = sent.astype(BF16)
    send_ref[BOT : BOT + HALF, :] = jnp.zeros((HALF, FEAT), BF16)
    send_ref[BOT : BOT + HALF, 0:LANE] = high
    send_ref[BOT : BOT + HALF, LANE : 2 * LANE] = (sent - high.astype(F32)).astype(BF16)


def two_terms(row):
    high = row.astype(BF16).astype(F32)
    rows = lax.broadcasted_iota(jnp.int32, (HALF, LANE), 0)
    block = jnp.where(rows == 0, high, jnp.where(rows == 1, row - high, 0.0))
    return block.astype(BF16)


def paired_kernel(
    keep_a_ref, got_a_ref, keep_b_ref, got_b_ref, extra_ref, keep_sum_ref, out_ref, sum_ref
):
    total = keep_sum_ref[...]
    for start in (0, ATT):
        term = got_a_ref[ATT : ATT + HALF, start : start + ATT].astype(F32)
        total = total + term[0:1, :]
    sum_ref[0:1, :] = total[:, 0:LANE]
    sum_ref[1:2, :] = total[:, LANE : 2 * LANE]
    sum_ref[2:8, :] = jnp.zeros((6, LANE), F32)
    for p in range(N_PLANE):
        at = slice(HALF * p, HALF * (p + 1))
        for j in range(BLOCKS):
            lanes = slice(LANE * j, LANE * (j + 1))
            sum_a = keep_a_ref[at, lanes] + got_a_ref[at, lanes].astype(F32)
            sum_b = keep_b_ref[at, lanes] + got_b_ref[at, lanes].astype(F32)
            out_ref[p, PIECE * j : PIECE * j + HALF, :] = sum_a.astype(BF16)
            out_ref[p, PIECE * j + HALF : PIECE * (j + 1), :] = sum_b.astype(BF16)
        cols = slice(0, LANE), slice(LANE, 2 * LANE)
        small = extra_ref[p : p + 1, :]
        for col in cols:
            small = small + got_b_ref[BOT : BOT + HALF, col].astype(F32)[p : p + 1, :]
        out_ref[p, MAIN:TALL, :] = two_terms(small)


def small_row(block):
    return block[MAIN : MAIN + 1, :].astype(F32) + block[MAIN + 1 : MAIN + 2, :].astype(F32)


def tail_parts(ref):
    tail = ref[MAIN:TALL, :].astype(F32)
    return tail[0:1] + tail[1:2], tail[2:10], tail[10:12] + tail[12:14]


def tail_block(small, profile, sums):
    high = small.astype(BF16).astype(F32)
    sums_high = sums.astype(BF16).astype(F32)
    rows = [high, small - high, profile, sums_high, sums - sums_high, jnp.zeros((2, LANE), F32)]
    return jnp.concatenate(rows, axis=0).astype(BF16)


def plane_sum_kernel(got_ref, profile_ref, sum_ref, out_ref):
    total = got_ref[0].astype(F32)
    for p in range(1, N_PLANE):
        total = total + got_ref[p].astype(F32)
    out_ref[0:MAIN, :] = total[0:MAIN].astype(BF16)
    out_ref[MAIN:TALL, :] = tail_block(small_row(total), profile_ref[...], sum_ref[0:2, :])


def z_pair_kernel(mine_ref, other_ref, out_ref):
    total = mine_ref[0:MAIN, :].astype(F32) + other_ref[0:MAIN, :].astype(F32)
    out_ref[0:MAIN, :] = total.astype(BF16)
    small, profile, sums = tail_parts(mine_ref)
    small_o, _, sums_o = tail_parts(other_ref)
    out_ref[MAIN:TALL, :] = tail_block(small + small_o, profile, sums + sums_o)


def z_sum_kernel(mine_ref, near_ref, far_ref, cross_ref, out_ref):
    near = mine_ref[0:MAIN, :].astype(F32) + near_ref[0:MAIN, :].astype(F32)
    far = far_ref[0:MAIN, :].astype(F32) + cross_ref[0:MAIN, :].astype(F32)
    main = (near + far).astype(BF16)
    small, profile, sums = tail_parts(mine_ref)
    small_n, _, sums_n = tail_parts(near_ref)
    small_f, _, sums_f = tail_parts(far_ref)
    small_c, _, sums_c = tail_parts(cross_ref)
    small = (small + small_n) + (small_f + small_c)
    tail = tail_block(small, profile, (sums + sums_n) + (sums_f + sums_c))
    for p in range(N_PLANE):
        out_ref[p, 0:MAIN, :] = main
        out_ref[p, MAIN:TALL, :] = tail


def unpack_kernel(own, got_ref, *refs):
    up_hbm, down_hbm, v_hbm, u_hbm, gup_hbm, gdown_hbm, aw_hbm = refs[-14:-7]
    attn_ref, down_ref, up_ref, gup_ref, gdown_ref, aw_ref, sems = refs[-7:]
    first = (lax.axis_index("core") == 0) if own else (lax.axis_index("core") != 0)
    to_v = pltpu.make_async_copy(attn_ref, v_hbm, sems.at[0])
    to_u = pltpu.make_async_copy(attn_ref, u_hbm, sems.at[0])
    to_down = pltpu.make_async_copy(down_ref, down_hbm, sems.at[1])
    to_up = pltpu.make_async_copy(up_ref, up_hbm, sems.at[1])
    smalls = [
        pltpu.make_async_copy(gup_ref, gup_hbm, sems.at[2]),
        pltpu.make_async_copy(gdown_ref, gdown_hbm, sems.at[3]),
        pltpu.make_async_copy(aw_ref, aw_hbm, sems.at[4]),
    ]
    tails = [got_ref[p, MAIN:TALL, :].astype(F32) for p in range(N_PLANE)]
    sums = [tail[10:12] + tail[12:14] for tail in tails]
    sums = [jnp.concatenate([v[0:1], v[1:2]], axis=1) for v in sums]
    sums = jnp.concatenate(split3(jnp.concatenate(sums, axis=0)), axis=0)
    for j in range(BLOCKS):
        rows = slice(PIECE * j, PIECE * j + HALF)
        attn = got_ref[:, rows, :].astype(F32).reshape(ATT, LANE)
        profile = jnp.concatenate([tail[2 + j : 3 + j] for tail in tails], axis=0).astype(BF16)
        outer = tn(jnp.concatenate([profile, profile, profile], axis=0), sums)
        attn_ref[LANE * j : LANE * (j + 1), :] = attn.T + outer

    @pl.when(first)
    def _():
        to_v.start()
        for j in range(BLOCKS):
            rows = slice(PIECE * j + HALF, PIECE * (j + 1))
            enc = got_ref[:, rows, :].astype(F32).reshape(BOT, LANE)
            down_ref[:, LANE * j : LANE * (j + 1)] = enc
        to_down.start()
        for r in range(12):
            block = got_ref[r, MAIN:TALL, :].astype(F32)
            small = block[0:1, :] + block[1:2, :]
            if r < 8:
                gdown_ref[:, LANE * r : LANE * (r + 1)] = small
            elif r < 10:
                aw_ref[:, LANE * (r - 8) : LANE * (r - 7)] = small
            else:
                gup_ref[:, LANE * (r - 10) : LANE * (r - 9)] = small
        for copy in smalls:
            copy.start()
        to_v.wait()
        to_down.wait()
        for copy in smalls:
            copy.wait()

    @pl.when(jnp.logical_not(first))
    def _():
        to_u.start()
        for j in range(BLOCKS):
            rows = slice(PIECE * j + HALF, PIECE * (j + 1))
            enc = got_ref[:, rows, :].astype(F32).reshape(BOT, LANE)
            up_ref[LANE * j : LANE * (j + 1), :] = enc.T
        to_up.start()
        to_u.wait()
        to_up.wait()


def whole_spec(shape):
    return pl.BlockSpec(shape, lambda *_: (0,) * len(shape))


def call(body, outs, *args, name):
    return pl.pallas_call(
        body,
        out_shape=[jax.ShapeDtypeStruct(s, d) for s, d in outs],
        compiler_params=params(),
        name=name,
    )(*args)


def swap(v, axis):
    return lax.ppermute(v, axis, [(0, 1), (1, 0)])


def in_hbm(*arrays):
    return [pltpu.with_memory_space_constraint(v, pltpu.HBM) for v in arrays]


def reduce_all(keep_a, got_a, keep_b, got_b, extra, keep_sum, profile):
    pieces = (N_PLANE, TALL, LANE)
    paired, sums = call(
        paired_kernel,
        [(pieces, BF16), ((8, LANE), F32)],
        keep_a, got_a, keep_b, got_b, extra, keep_sum,
        name="paired",
    )
    got = lax.all_to_all(paired, PLANE, 0, 0, tiled=True)
    flat = [(pieces[1:], BF16)]
    (part,) = call(plane_sum_kernel, flat, got, profile, sums, name="plane_sum")
    (pair,) = call(z_pair_kernel, flat, part, cross_z(part, 1), name="z_pair")
    (whole,) = call(
        z_sum_kernel,
        [(pieces, BF16)],
        pair, cross_z(pair, 2), cross_z(pair, 4), cross_z(pair, 6),
        name="z_sum",
    )
    return lax.all_to_all(whole, PLANE, 0, 0, tiled=True)


def cross_z(v, bits):
    return lax.ppermute(v, "z", [(i, i ^ bits) for i in range(N_Z)])


def unpack(got, *before):
    hbm = pl.BlockSpec(memory_space=pltpu.HBM)
    shapes = [
        (FEAT, BOT), (BOT, FEAT), (FEAT, ATT), (FEAT, ATT), (1, BOT), (1, FEAT), (1, ATT)
    ]
    return pl.pallas_call(
        functools.partial(unpack_kernel, not before),
        in_specs=[VMEM] + [hbm] * len(before),
        out_specs=[hbm] * len(shapes),
        out_shape=[jax.ShapeDtypeStruct(v, F32) for v in shapes],
        input_output_aliases={1 + i: i for i in range(len(before))},
        scratch_shapes=[
            pltpu.VMEM((FEAT, ATT), F32),
            pltpu.VMEM((BOT, FEAT), F32),
            pltpu.VMEM((FEAT, BOT), F32),
            pltpu.VMEM((1, BOT), F32),
            pltpu.VMEM((1, FEAT), F32),
            pltpu.VMEM((1, ATT), F32),
            pltpu.SemaphoreType.DMA((5,)),
        ],
        compiler_params=params(),
        name="unpack_other" if before else "unpack_own",
    )(got, *before)


def encode(
    rows, slide_ids, counts, pooled_cot, w_up, w_down, gu, gd, attn_v, attn_u, aw
):
    hbm = pl.BlockSpec(memory_space=pltpu.HBM)
    outs = [
        ((SLOTS * POS, FEAT), BF16),
        ((SLOTS * POS, BOT), BF16),
        ((SLOTS * POS, BOT), F32),
        ((SLOTS, FEAT), F32),
        ((SLOTS, ATT), F32),
        ((SLOTS, ATT), F32),
        ((SLOTS, LANE), F32),
        ((40, LANE), F32),
        ((1, SLOTS), jnp.int32),
        ((BOT, FEAT), BF16),
        ((1, BOT), F32),
        ((1, FEAT), F32),
        ((FEAT, ATT), BF16),
        ((FEAT, ATT), BF16),
        ((1, ATT), F32),
    ]
    return pl.pallas_call(
        forward_kernel,
        in_specs=[hbm] * 10 + [pl.BlockSpec(memory_space=pltpu.SMEM)],
        out_specs=[VMEM] * len(outs),
        out_shape=[jax.ShapeDtypeStruct(s, d) for s, d in outs],
        scratch_shapes=[
            pltpu.VMEM((FEAT, BOT), BF16),
            pltpu.VMEM((1, SLOTS), jnp.int32),
            pltpu.VMEM((4, 32), BF16),
            pltpu.SemaphoreType.DMA((len(LOADS) + 9,)),
        ],
        compiler_params=params(),
        name="encode",
    )(*in_hbm(rows, w_up, w_down, gu, gd, attn_v, attn_u, aw, slide_ids, pooled_cot), counts)


def backward_rows(mask, up, back, small, w_down, gu):
    outs = [((SLOTS * POS, FEAT), BF16), ((SLOTS * POS, BOT), BF16), ((HALF, LANE), F32)]
    return call(rows_kernel, outs, mask, up, back, small, w_down, gu, name="backward_rows")


def backward_sums(x, hid, dback, dup, small):
    outs = [((BOT, FEAT), F32), ((BOT + HALF, FEAT), BF16), ((HALF, LANE), F32)]
    return call(sums_kernel, outs, x, hid, dback, dup, small, name="backward_sums")


def per_device(
    tiles, counts, slide_ids, pooled_cot, w_up, w_down, gain_up, gain_down, attn_v, attn_u, attn_w
):
    rows = tiles.reshape(SLOTS * POS, FEAT)
    gu = gain_up.reshape(1, BOT)
    gd = gain_down.reshape(1, FEAT)
    aw = attn_w.reshape(1, ATT)
    x, hid, up, feat, tanh, sigm, weight, pack, ids, *loaded = encode(
        rows, slide_ids, counts, pooled_cot, w_up, w_down, gu, gd, attn_v, attn_u, aw
    )
    w_down, gu, gd, attn_v, attn_u, aw = loaded
    (half,) = call(pair_kernel, [((40, LANE), F32)], pack, swap(pack, "core"), name="pair")
    mask, act, slope = call(
        keep_kernel,
        [((SLOTS * POS, FEAT), BF16), ((SLOTS, FEAT), F32), ((SLOTS, FEAT), F32)],
        x, hid, w_down, gd, tanh, sigm, aw, attn_v, attn_u,
        name="keep",
    )
    across, mask, act, slope = lax.optimization_barrier((swap(half, "x_hi"), mask, act, slope))
    (spread,) = call(spread_kernel, [((N_Z, 48, LANE), F32)], half, across, name="spread")
    got = lax.all_to_all(spread, "z", 0, 0, tiled=True)

    back, pooled, small, keep_a, send_a, keep_sum, profile = pl.pallas_call(
        middle_kernel,
        in_specs=[VMEM] * 10,
        out_shape=[
            jax.ShapeDtypeStruct((SLOTS, FEAT), F32),
            jax.ShapeDtypeStruct((4, FEAT), F32),
            jax.ShapeDtypeStruct((16, LANE), F32),
            jax.ShapeDtypeStruct((ATT, FEAT), F32),
            jax.ShapeDtypeStruct((ATT + HALF, FEAT), BF16),
            jax.ShapeDtypeStruct((1, ATT), F32),
            jax.ShapeDtypeStruct((8, LANE), F32),
        ],
        compiler_params=params(),
        name="middle",
    )(ids, got, feat, act, slope, tanh, sigm, weight, aw, gd)

    dback, dup, small = backward_rows(mask, up, back, small, w_down, gu)
    got_a, dback = lax.optimization_barrier((swap(send_a, "core"), dback))
    keep_b, send_b, extra = backward_sums(x, hid, dback, dup, small)
    got_b = swap(send_b, "core")

    mine = reduce_all(keep_a, got_a, keep_b, got_b, extra, keep_sum, profile)
    other = swap(mine, "core")
    g_up, g_down, g_v, g_u, g_gu, g_gd, g_aw = unpack(other, *unpack(mine))
    return (
        pooled,
        g_up,
        g_down,
        g_gu.reshape(BOT),
        g_gd.reshape(FEAT),
        g_v,
        g_u,
        g_aw.reshape(ATT),
    )


def solution(mesh):
    fine = Mesh(mesh.devices.reshape(2, 4, 2, 8, 2), FINE)
    return jax.shard_map(
        per_device,
        mesh=fine,
        in_specs=(
            P(SLIDE, TILE, None, None),
            P(SLIDE, TILE),
            P(SLIDE, TILE),
            P(SLIDE, TILE),
            P(),
            P(),
            P(),
            P(),
            P(),
            P(),
            P(),
        ),
        out_specs=(P(SLIDE, None), P(), P(), P(), P(), P(), P(), P()),
        check_vma=False,
    )
```

```python
import functools

import jax
import jax.numpy as jnp
from jax import lax
from jax.experimental import pallas as pl
from jax.experimental.pallas import tpu as pltpu
from jax.sharding import Mesh
from jax.sharding import PartitionSpec as P

F32 = jnp.float32
BF16 = jnp.bfloat16

FINE = ("x_lo", "y", "x_hi", "z", "core")
SLIDE = ("x_lo", "y")
TILE = ("x_hi", "z", "core")
PLANE = ("x_lo", "y", "x_hi")
N_PLANE = 16
N_Z = 8

SLOTS = 32
POS = 64
FEAT = 1024
BOT = 256
ATT = 256
LANE = 128
STEPS = 4
GROUP = SLOTS // STEPS
PIECE = 32
HALF = 16
BLOCKS = FEAT // LANE
MAIN = PIECE * BLOCKS
TALL = MAIN + HALF
ROWS = GROUP * POS

CHUNKS = 8
CHUNK = SLOTS * POS // CHUNKS
LOADS = (512, 1536)

VMEM_LIMIT = 24 * 1024 * 1024
VMEM = pl.BlockSpec(memory_space=pltpu.VMEM)


def params():
    return pltpu.CompilerParams(vmem_limit_bytes=VMEM_LIMIT)


def nn(a, b):
    return jnp.dot(a, b, preferred_element_type=F32)


def nt(a, b):
    return lax.dot_general(a, b, (((1,), (1,)), ((), ())), preferred_element_type=F32)


def tn(a, b):
    return lax.dot_general(a, b, (((0,), (0,)), ((), ())), preferred_element_type=F32)


def sigmoid(v):
    return 1.0 / (1.0 + jnp.exp(-v))


def column(row):
    n = row.shape[1]
    i = lax.broadcasted_iota(jnp.int32, (n, n), 0)
    j = lax.broadcasted_iota(jnp.int32, (n, n), 1)
    return jnp.sum(jnp.where(i == j, jnp.broadcast_to(row, (n, n)), 0), axis=1, keepdims=True)


def members(ids_ref):
    ids = column(ids_ref[...])
    return [ids == c for c in range(4)], ids >= 0


def split3(v):
    hi = v.astype(BF16)
    rest = v - hi.astype(F32)
    mid = rest.astype(BF16)
    low = (rest - mid.astype(F32)).astype(BF16)
    return [hi, mid, low]


def slopes(tanh, sigm, aw):
    return aw * sigm * (1.0 - tanh * tanh), aw * tanh * sigm * (1.0 - sigm)


def forward_kernel(
    x_hbm, wu_hbm, wd_hbm, gu_hbm, gd_hbm, av_hbm, au_hbm, aw_hbm, ids_hbm, cot_hbm, count_ref,
    x_ref, hid_ref, up_ref, feat_ref, tanh_ref, sigm_ref, weight_ref, pack_ref, live_ref,
    wd_ref, gu_ref, gd_ref, av_ref, au_ref, aw_ref, wu_ref, ids_ref, cot_ref, sems,
):
    starts = [sum(LOADS[:i]) for i in range(len(LOADS))]
    loads = []
    for i, start in enumerate(starts):
        at = pl.ds(start, LOADS[i])
        loads.append(pltpu.make_async_copy(x_hbm.at[at, :], x_ref.at[at, :], sems.at[i]))
    pairs = [
        (wu_hbm, wu_ref),
        (gu_hbm, gu_ref),
        (wd_hbm, wd_ref),
        (gd_hbm, gd_ref),
        (av_hbm, av_ref),
        (au_hbm, au_ref),
        (aw_hbm, aw_ref),
        (ids_hbm, ids_ref),
        (cot_hbm, cot_ref),
    ]
    others = [
        pltpu.make_async_copy(src, dst, sems.at[len(LOADS) + i])
        for i, (src, dst) in enumerate(pairs)
    ]
    others[0].start()
    loads[0].start()
    for copy in others[1:4]:
        copy.start()
    for copy in loads[1:]:
        copy.start()
    for copy in others[4:]:
        copy.start()
    for copy in others[:4]:
        copy.wait()
    for i in range(CHUNKS):
        at = slice(i * CHUNK, (i + 1) * CHUNK)
        if i * CHUNK in starts:
            loads[starts.index(i * CHUNK)].wait()
        x = x_ref[at, :]
        up = nn(x, wu_ref[...])
        up_ref[at, :] = up
        hidden = jnp.maximum(up * gu_ref[...], 0.0).astype(BF16)
        hid_ref[at, :] = hidden
        down = nn(hidden, wd_ref[...])
        res = x.astype(F32) + down * gd_ref[...]
        feats = jnp.sum(jnp.maximum(res, 0.0).reshape(CHUNK // POS, POS, FEAT), axis=1)
        feat_ref[i * CHUNK // POS : (i + 1) * CHUNK // POS, :] = feats * (1.0 / POS)
    for copy in others[4:]:
        copy.wait()
    feat = feat_ref[...]
    feat_b = feat.astype(BF16)
    tanh = jnp.tanh(nn(feat_b, av_ref[...]))
    sigm = sigmoid(nn(feat_b, au_ref[...]))
    tanh_ref[...] = tanh
    sigm_ref[...] = sigm
    weight = sigmoid(jnp.sum(tanh * sigm * aw_ref[...], axis=1, keepdims=True))
    weight_ref[...] = jnp.broadcast_to(weight, (SLOTS, LANE))
    slot = lax.broadcasted_iota(jnp.int32, (1, SLOTS), 1)
    live_ref[...] = jnp.where(slot < count_ref[0, 0], ids_ref[...], -1)
    member, _ = members(live_ref)
    for c in range(4):
        share = jnp.where(member[c], weight, 0.0)
        num = jnp.sum(share * feat, axis=0, keepdims=True)
        den = jnp.sum(share, axis=0, keepdims=True)
        for r in range(8):
            pack_ref[8 * c + r : 8 * c + r + 1, :] = num[:, LANE * r : LANE * (r + 1)]
        pack_ref[36 + c : 37 + c, :] = jnp.broadcast_to(den, (1, LANE))
    quarter = lax.rem(lax.axis_index("z"), 2) * 2 + lax.axis_index("core")
    lane = lax.broadcasted_iota(jnp.int32, (4, LANE), 1)
    mine = jnp.logical_and(lane >= quarter * 32, lane < quarter * 32 + 32)
    cot = cot_ref[...].astype(F32)
    cot = jnp.concatenate([cot, cot, cot, cot], axis=1)
    pack_ref[32:36, :] = jnp.where(mine, cot, 0.0)


def keep_kernel(
    x_ref, hid_ref, wd_ref, gd_ref, tanh_ref, sigm_ref, aw_ref, av_ref, au_ref,
    mask_ref, act_ref, slope_ref,
):
    for i in range(CHUNKS):
        at = slice(i * CHUNK, (i + 1) * CHUNK)
        down = nn(hid_ref[at, :], wd_ref[...])
        positive = x_ref[at, :].astype(F32) + down * gd_ref[...] > 0
        mask_ref[at, :] = jnp.where(positive, 1.0, 0.0).astype(BF16)
        acts = jnp.where(positive, down, 0.0).reshape(CHUNK // POS, POS, FEAT)
        act_ref[i * CHUNK // POS : (i + 1) * CHUNK // POS, :] = jnp.sum(acts, axis=1)
    slope_t, slope_s = slopes(tanh_ref[...], sigm_ref[...], aw_ref[...])
    from_t = nt(jnp.concatenate(split3(slope_t), axis=0), av_ref[...])
    from_s = nt(jnp.concatenate(split3(slope_s), axis=0), au_ref[...])
    total = from_t[0:32] + from_t[32:64] + from_t[64:96]
    slope_ref[...] = total + (from_s[0:32] + from_s[32:64] + from_s[64:96])


def pair_kernel(mine_ref, other_ref, out_ref):
    out_ref[...] = mine_ref[...] + other_ref[...]


def spread_kernel(mine_ref, other_ref, out_ref):
    first = lax.axis_index("x_hi") == 0
    mine = mine_ref[...]
    other = other_ref[...]
    low = jnp.where(first, mine, other)[32:36]
    high = jnp.where(first, other, mine)[32:36]
    out = mine + other
    for p in range(N_Z):
        out_ref[p, 0:32, :] = out[0:32]
        out_ref[p, 32:36, :] = low + pltpu.roll(high, LANE // 2, 1)
        out_ref[p, 36:40, :] = out[36:40]


def middle_kernel(
    ids_ref, got_ref, feat_ref, act_ref, slope_ref, tanh_ref, sigm_ref, weight_ref,
    aw_ref, gd_ref,
    back_ref, pooled_ref, small_ref, keep_ref, send_ref, keep_sum_ref, profile_ref,
):
    core = lax.axis_index("core")
    total = got_ref[0]
    for p in range(1, N_Z):
        total = total + got_ref[p]
    even = lax.broadcasted_iota(jnp.int32, (4, LANE), 1) < LANE // 2
    cots = [got_ref[p, 32:36, :] for p in range(N_Z)]
    lows = [jnp.where(even, cots[p], cots[p + 1]) for p in range(0, N_Z, 2)]
    highs = [
        pltpu.roll(jnp.where(even, cots[p + 1], cots[p]), LANE // 2, 1) for p in range(0, N_Z, 2)
    ]
    cot = jnp.concatenate(lows + highs, axis=1)
    member, live = members(ids_ref)
    cot_tile = jnp.zeros((SLOTS, FEAT), F32)
    pooled_tile = jnp.zeros((SLOTS, FEAT), F32)
    den_tile = jnp.where(live, 0.0, 1.0)
    profile = jnp.zeros((1, FEAT), F32)
    for c in range(4):
        num = jnp.concatenate([total[8 * c + r : 8 * c + r + 1, :] for r in range(8)], axis=1)
        den = total[36 + c : 37 + c, 0:1]
        pooled = num / den
        pooled_ref[c : c + 1, :] = pooled
        profile = profile + pooled
        cot_tile = jnp.where(member[c], cot[c : c + 1, :], cot_tile)
        pooled_tile = jnp.where(member[c], pooled, pooled_tile)
        den_tile = jnp.where(member[c], den, den_tile)
    feat = feat_ref[...]
    tanh = tanh_ref[...]
    sigm = sigm_ref[...]
    weight = weight_ref[:, 0:1]
    aw = aw_ref[...]
    dweight = jnp.sum(cot_tile * (feat - pooled_tile), axis=1, keepdims=True) / den_tile
    dscore = dweight * weight * (1.0 - weight)
    grad_aw = jnp.sum(dscore * tanh * sigm, axis=0, keepdims=True)
    slope_t, slope_s = slopes(tanh, sigm, aw)
    grad_t = dscore * slope_t
    grad_s = dscore * slope_s
    profile = (profile * 0.25).astype(BF16).astype(F32)
    norm = jnp.maximum(jnp.sum(profile * profile, axis=1, keepdims=True), 1e-30)
    feat_b = feat.astype(BF16).astype(F32)
    along = jnp.sum(feat_b * profile, axis=1, keepdims=True) / norm
    rest = feat_b - along * profile
    rest_0, rest_1, _ = split3(rest)
    rest_3 = jnp.concatenate([rest_0, rest_0, rest_1], axis=0)
    grad_t0, grad_t1, _ = split3(grad_t)
    grad_s0, grad_s1, _ = split3(grad_s)
    grad_v = tn(jnp.concatenate([grad_t0, grad_t1, grad_t0], axis=0), rest_3)
    grad_u = tn(jnp.concatenate([grad_s0, grad_s1, grad_s0], axis=0), rest_3)
    sum_t = jnp.sum(along * grad_t, axis=0, keepdims=True)
    sum_s = jnp.sum(along * grad_s, axis=0, keepdims=True)
    for r in range(8):
        profile_ref[r : r + 1, :] = profile[:, LANE * r : LANE * (r + 1)]
    keep_sum_ref[...] = jnp.where(core == 0, sum_t, sum_s)
    sent = jnp.where(core == 0, sum_s, sum_t)
    high = sent.astype(BF16)
    send_ref[ATT : ATT + HALF, :] = jnp.zeros((HALF, FEAT), BF16)
    send_ref[ATT : ATT + HALF, 0:ATT] = jnp.broadcast_to(high, (HALF, ATT))
    low = (sent - high.astype(F32)).astype(BF16)
    send_ref[ATT : ATT + HALF, ATT : 2 * ATT] = jnp.broadcast_to(low, (HALF, ATT))

    @pl.when(core == 0)
    def _():
        keep_ref[...] = grad_v
        send_ref[0:ATT, :] = grad_u.astype(BF16)

    @pl.when(core != 0)
    def _():
        keep_ref[...] = grad_u
        send_ref[0:ATT, :] = grad_v.astype(BF16)

    dfeat = ((weight / den_tile) * cot_tile + dscore * slope_ref[...]) * (1.0 / POS)
    back_ref[...] = (dfeat * gd_ref[...]).astype(BF16).astype(F32)
    grad_gd = jnp.sum(dfeat * act_ref[...], axis=0, keepdims=True)
    for r in range(8):
        small_ref[r : r + 1, :] = grad_gd[:, LANE * r : LANE * (r + 1)]
    for r in range(2):
        small_ref[8 + r : 9 + r, :] = grad_aw[:, LANE * r : LANE * (r + 1)]
    small_ref[10:16, :] = jnp.zeros((6, LANE), F32)


def rows_kernel(
    mask_ref, up_ref, back_ref, small_ref, wd_ref, gu_ref, dback_ref, dup_ref, out_ref
):
    gu = gu_ref[...]
    gain = jnp.zeros((8, BOT), F32)
    for i in range(STEPS):
        at = slice(ROWS * i, ROWS * (i + 1))
        for k in range(GROUP):
            tile = GROUP * i + k
            row = back_ref[tile : tile + 1, :].astype(BF16)
            here = slice(POS * tile, POS * (tile + 1))
            dback_ref[here, :] = mask_ref[here, :] * jnp.broadcast_to(row, (POS, FEAT))
        dhid = nt(dback_ref[at, :], wd_ref[...])
        up = up_ref[at, :]
        dscaled = jnp.where(up * gu > 0, dhid, 0.0)
        gain = gain + jnp.sum((dscaled * up).reshape(ROWS // 8, 8, BOT), axis=0)
        dup_ref[at, :] = (dscaled * gu).astype(BF16)
    gain = jnp.sum(gain, axis=0, keepdims=True)
    out_ref[0:10, :] = small_ref[0:10, :]
    out_ref[10:11, :] = gain[:, 0:LANE]
    out_ref[11:12, :] = gain[:, LANE : 2 * LANE]
    out_ref[12:HALF, :] = jnp.zeros((HALF - 12, LANE), F32)


def sums_kernel(x_ref, hid_ref, dback_ref, dup_ref, small_ref, keep_ref, send_ref, extra_ref):
    small = small_ref[...]
    first = lax.axis_index("core") == 0
    down = tn(hid_ref[...], dback_ref[...])
    up_grad = tn(dup_ref[...], x_ref[...])

    @pl.when(first)
    def _():
        keep_ref[...] = down
        extra_ref[...] = small
        send_ref[0:BOT, :] = up_grad.astype(BF16)

    @pl.when(jnp.logical_not(first))
    def _():
        keep_ref[...] = up_grad
        extra_ref[...] = jnp.zeros((HALF, LANE), F32)
        send_ref[0:BOT, :] = down.astype(BF16)

    sent = jnp.where(first, 0.0, small)
    high = sent.astype(BF16)
    send_ref[BOT : BOT + HALF, :] = jnp.zeros((HALF, FEAT), BF16)
    send_ref[BOT : BOT + HALF, 0:LANE] = high
    send_ref[BOT : BOT + HALF, LANE : 2 * LANE] = (sent - high.astype(F32)).astype(BF16)


def two_terms(row):
    high = row.astype(BF16).astype(F32)
    rows = lax.broadcasted_iota(jnp.int32, (HALF, LANE), 0)
    block = jnp.where(rows == 0, high, jnp.where(rows == 1, row - high, 0.0))
    return block.astype(BF16)


def paired_kernel(
    keep_a_ref, got_a_ref, keep_b_ref, got_b_ref, extra_ref, keep_sum_ref, out_ref, sum_ref
):
    total = keep_sum_ref[...]
    for start in (0, ATT):
        term = got_a_ref[ATT : ATT + HALF, start : start + ATT].astype(F32)
        total = total + term[0:1, :]
    sum_ref[0:1, :] = total[:, 0:LANE]
    sum_ref[1:2, :] = total[:, LANE : 2 * LANE]
    sum_ref[2:8, :] = jnp.zeros((6, LANE), F32)
    for p in range(N_PLANE):
        at = slice(HALF * p, HALF * (p + 1))
        for j in range(BLOCKS):
            lanes = slice(LANE * j, LANE * (j + 1))
            sum_a = keep_a_ref[at, lanes] + got_a_ref[at, lanes].astype(F32)
            sum_b = keep_b_ref[at, lanes] + got_b_ref[at, lanes].astype(F32)
            out_ref[p, PIECE * j : PIECE * j + HALF, :] = sum_a.astype(BF16)
            out_ref[p, PIECE * j + HALF : PIECE * (j + 1), :] = sum_b.astype(BF16)
        cols = slice(0, LANE), slice(LANE, 2 * LANE)
        small = extra_ref[p : p + 1, :]
        for col in cols:
            small = small + got_b_ref[BOT : BOT + HALF, col].astype(F32)[p : p + 1, :]
        out_ref[p, MAIN:TALL, :] = two_terms(small)


def small_row(block):
    return block[MAIN : MAIN + 1, :].astype(F32) + block[MAIN + 1 : MAIN + 2, :].astype(F32)


def tail_parts(ref):
    tail = ref[MAIN:TALL, :].astype(F32)
    return tail[0:1] + tail[1:2], tail[2:10], tail[10:12] + tail[12:14]


def tail_block(small, profile, sums):
    high = small.astype(BF16).astype(F32)
    sums_high = sums.astype(BF16).astype(F32)
    rows = [high, small - high, profile, sums_high, sums - sums_high, jnp.zeros((2, LANE), F32)]
    return jnp.concatenate(rows, axis=0).astype(BF16)


def plane_sum_kernel(got_ref, profile_ref, sum_ref, out_ref):
    total = got_ref[0].astype(F32)
    for p in range(1, N_PLANE):
        total = total + got_ref[p].astype(F32)
    out_ref[0:MAIN, :] = total[0:MAIN].astype(BF16)
    out_ref[MAIN:TALL, :] = tail_block(small_row(total), profile_ref[...], sum_ref[0:2, :])


def z_pair_kernel(mine_ref, other_ref, out_ref):
    total = mine_ref[0:MAIN, :].astype(F32) + other_ref[0:MAIN, :].astype(F32)
    out_ref[0:MAIN, :] = total.astype(BF16)
    small, profile, sums = tail_parts(mine_ref)
    small_o, _, sums_o = tail_parts(other_ref)
    out_ref[MAIN:TALL, :] = tail_block(small + small_o, profile, sums + sums_o)


def z_sum_kernel(mine_ref, near_ref, cross_ref, far_ref, out_ref):
    near = mine_ref[0:MAIN, :].astype(F32) + near_ref[0:MAIN, :].astype(F32)
    far = far_ref[0:MAIN, :].astype(F32) + cross_ref[0:MAIN, :].astype(F32)
    main = (near + far).astype(BF16)
    small, profile, sums = tail_parts(mine_ref)
    small_n, _, sums_n = tail_parts(near_ref)
    small_f, _, sums_f = tail_parts(far_ref)
    small_c, _, sums_c = tail_parts(cross_ref)
    small = (small + small_n) + (small_f + small_c)
    tail = tail_block(small, profile, (sums + sums_n) + (sums_f + sums_c))
    for p in range(N_PLANE):
        out_ref[p, 0:MAIN, :] = main
        out_ref[p, MAIN:TALL, :] = tail


def unpack_kernel(own, got_ref, *refs):
    up_hbm, down_hbm, v_hbm, u_hbm, gup_hbm, gdown_hbm, aw_hbm = refs[-14:-7]
    attn_ref, down_ref, up_ref, gup_ref, gdown_ref, aw_ref, sems = refs[-7:]
    first = (lax.axis_index("core") == 0) if own else (lax.axis_index("core") != 0)
    to_v = pltpu.make_async_copy(attn_ref, v_hbm, sems.at[0])
    to_u = pltpu.make_async_copy(attn_ref, u_hbm, sems.at[0])
    to_down = pltpu.make_async_copy(down_ref, down_hbm, sems.at[1])
    to_up = pltpu.make_async_copy(up_ref, up_hbm, sems.at[1])
    smalls = [
        pltpu.make_async_copy(gup_ref, gup_hbm, sems.at[2]),
        pltpu.make_async_copy(gdown_ref, gdown_hbm, sems.at[3]),
        pltpu.make_async_copy(aw_ref, aw_hbm, sems.at[4]),
    ]
    tails = [got_ref[p, MAIN:TALL, :].astype(F32) for p in range(N_PLANE)]
    sums = [tail[10:12] + tail[12:14] for tail in tails]
    sums = [jnp.concatenate([v[0:1], v[1:2]], axis=1) for v in sums]
    sums = jnp.concatenate(split3(jnp.concatenate(sums, axis=0)), axis=0)
    for j in range(BLOCKS):
        rows = slice(PIECE * j, PIECE * j + HALF)
        attn = got_ref[:, rows, :].astype(F32).reshape(ATT, LANE)
        profile = jnp.concatenate([tail[2 + j : 3 + j] for tail in tails], axis=0).astype(BF16)
        outer = tn(jnp.concatenate([profile, profile, profile], axis=0), sums)
        attn_ref[LANE * j : LANE * (j + 1), :] = attn.T + outer

    @pl.when(first)
    def _():
        to_v.start()
        for j in range(BLOCKS):
            rows = slice(PIECE * j + HALF, PIECE * (j + 1))
            enc = got_ref[:, rows, :].astype(F32).reshape(BOT, LANE)
            down_ref[:, LANE * j : LANE * (j + 1)] = enc
        to_down.start()
        for r in range(12):
            block = got_ref[r, MAIN:TALL, :].astype(F32)
            small = block[0:1, :] + block[1:2, :]
            if r < 8:
                gdown_ref[:, LANE * r : LANE * (r + 1)] = small
            elif r < 10:
                aw_ref[:, LANE * (r - 8) : LANE * (r - 7)] = small
            else:
                gup_ref[:, LANE * (r - 10) : LANE * (r - 9)] = small
        for copy in smalls:
            copy.start()
        to_v.wait()
        to_down.wait()
        for copy in smalls:
            copy.wait()

    @pl.when(jnp.logical_not(first))
    def _():
        to_u.start()
        for j in range(BLOCKS):
            rows = slice(PIECE * j + HALF, PIECE * (j + 1))
            enc = got_ref[:, rows, :].astype(F32).reshape(BOT, LANE)
            up_ref[LANE * j : LANE * (j + 1), :] = enc.T
        to_up.start()
        to_u.wait()
        to_up.wait()


def whole_spec(shape):
    return pl.BlockSpec(shape, lambda *_: (0,) * len(shape))


def call(body, outs, *args, name):
    return pl.pallas_call(
        body,
        out_shape=[jax.ShapeDtypeStruct(s, d) for s, d in outs],
        compiler_params=params(),
        name=name,
    )(*args)


def swap(v, axis):
    return lax.ppermute(v, axis, [(0, 1), (1, 0)])


def in_hbm(*arrays):
    return [pltpu.with_memory_space_constraint(v, pltpu.HBM) for v in arrays]


def reduce_all(keep_a, got_a, keep_b, got_b, extra, keep_sum, profile):
    pieces = (N_PLANE, TALL, LANE)
    paired, sums = call(
        paired_kernel,
        [(pieces, BF16), ((8, LANE), F32)],
        keep_a, got_a, keep_b, got_b, extra, keep_sum,
        name="paired",
    )
    got = lax.all_to_all(paired, PLANE, 0, 0, tiled=True)
    flat = [(pieces[1:], BF16)]
    (part,) = call(plane_sum_kernel, flat, got, profile, sums, name="plane_sum")
    (pair,) = call(z_pair_kernel, flat, part, cross_z(part, 1), name="z_pair")
    near, cross, far = [cross_z(pair, bits) for bits in (2, 6, 4)]
    (whole,) = call(
        z_sum_kernel,
        [(pieces, BF16)],
        pair, near, cross, far,
        name="z_sum",
    )
    return lax.all_to_all(whole, PLANE, 0, 0, tiled=True)


def cross_z(v, bits):
    return lax.ppermute(v, "z", [(i, i ^ bits) for i in range(N_Z)])


def unpack(got, *before):
    hbm = pl.BlockSpec(memory_space=pltpu.HBM)
    shapes = [
        (FEAT, BOT), (BOT, FEAT), (FEAT, ATT), (FEAT, ATT), (1, BOT), (1, FEAT), (1, ATT)
    ]
    return pl.pallas_call(
        functools.partial(unpack_kernel, not before),
        in_specs=[VMEM] + [hbm] * len(before),
        out_specs=[hbm] * len(shapes),
        out_shape=[jax.ShapeDtypeStruct(v, F32) for v in shapes],
        input_output_aliases={1 + i: i for i in range(len(before))},
        scratch_shapes=[
            pltpu.VMEM((FEAT, ATT), F32),
            pltpu.VMEM((BOT, FEAT), F32),
            pltpu.VMEM((FEAT, BOT), F32),
            pltpu.VMEM((1, BOT), F32),
            pltpu.VMEM((1, FEAT), F32),
            pltpu.VMEM((1, ATT), F32),
            pltpu.SemaphoreType.DMA((5,)),
        ],
        compiler_params=params(),
        name="unpack_other" if before else "unpack_own",
    )(got, *before)


def encode(
    rows, slide_ids, counts, pooled_cot, w_up, w_down, gu, gd, attn_v, attn_u, aw
):
    hbm = pl.BlockSpec(memory_space=pltpu.HBM)
    outs = [
        ((SLOTS * POS, FEAT), BF16),
        ((SLOTS * POS, BOT), BF16),
        ((SLOTS * POS, BOT), F32),
        ((SLOTS, FEAT), F32),
        ((SLOTS, ATT), F32),
        ((SLOTS, ATT), F32),
        ((SLOTS, LANE), F32),
        ((40, LANE), F32),
        ((1, SLOTS), jnp.int32),
        ((BOT, FEAT), BF16),
        ((1, BOT), F32),
        ((1, FEAT), F32),
        ((FEAT, ATT), BF16),
        ((FEAT, ATT), BF16),
        ((1, ATT), F32),
    ]
    return pl.pallas_call(
        forward_kernel,
        in_specs=[hbm] * 10 + [pl.BlockSpec(memory_space=pltpu.SMEM)],
        out_specs=[VMEM] * len(outs),
        out_shape=[jax.ShapeDtypeStruct(s, d) for s, d in outs],
        scratch_shapes=[
            pltpu.VMEM((FEAT, BOT), BF16),
            pltpu.VMEM((1, SLOTS), jnp.int32),
            pltpu.VMEM((4, 32), BF16),
            pltpu.SemaphoreType.DMA((len(LOADS) + 9,)),
        ],
        compiler_params=params(),
        name="encode",
    )(*in_hbm(rows, w_up, w_down, gu, gd, attn_v, attn_u, aw, slide_ids, pooled_cot), counts)


def backward_rows(mask, up, back, small, w_down, gu):
    outs = [((SLOTS * POS, FEAT), BF16), ((SLOTS * POS, BOT), BF16), ((HALF, LANE), F32)]
    return call(rows_kernel, outs, mask, up, back, small, w_down, gu, name="backward_rows")


def backward_sums(x, hid, dback, dup, small):
    outs = [((BOT, FEAT), F32), ((BOT + HALF, FEAT), BF16), ((HALF, LANE), F32)]
    return call(sums_kernel, outs, x, hid, dback, dup, small, name="backward_sums")


def per_device(
    tiles, counts, slide_ids, pooled_cot, w_up, w_down, gain_up, gain_down, attn_v, attn_u, attn_w
):
    rows = tiles.reshape(SLOTS * POS, FEAT)
    gu = gain_up.reshape(1, BOT)
    gd = gain_down.reshape(1, FEAT)
    aw = attn_w.reshape(1, ATT)
    x, hid, up, feat, tanh, sigm, weight, pack, ids, *loaded = encode(
        rows, slide_ids, counts, pooled_cot, w_up, w_down, gu, gd, attn_v, attn_u, aw
    )
    w_down, gu, gd, attn_v, attn_u, aw = loaded
    (half,) = call(pair_kernel, [((40, LANE), F32)], pack, swap(pack, "core"), name="pair")
    mask, act, slope = call(
        keep_kernel,
        [((SLOTS * POS, FEAT), BF16), ((SLOTS, FEAT), F32), ((SLOTS, FEAT), F32)],
        x, hid, w_down, gd, tanh, sigm, aw, attn_v, attn_u,
        name="keep",
    )
    across, mask, act, slope = lax.optimization_barrier((swap(half, "x_hi"), mask, act, slope))
    (spread,) = call(spread_kernel, [((N_Z, 40, LANE), F32)], half, across, name="spread")
    got = lax.all_to_all(spread, "z", 0, 0, tiled=True)

    back, pooled, small, keep_a, send_a, keep_sum, profile = pl.pallas_call(
        middle_kernel,
        in_specs=[VMEM] * 10,
        out_shape=[
            jax.ShapeDtypeStruct((SLOTS, FEAT), F32),
            jax.ShapeDtypeStruct((4, FEAT), F32),
            jax.ShapeDtypeStruct((16, LANE), F32),
            jax.ShapeDtypeStruct((ATT, FEAT), F32),
            jax.ShapeDtypeStruct((ATT + HALF, FEAT), BF16),
            jax.ShapeDtypeStruct((1, ATT), F32),
            jax.ShapeDtypeStruct((8, LANE), F32),
        ],
        compiler_params=params(),
        name="middle",
    )(ids, got, feat, act, slope, tanh, sigm, weight, aw, gd)

    dback, dup, small = backward_rows(mask, up, back, small, w_down, gu)
    got_a, dback = lax.optimization_barrier((swap(send_a, "core"), dback))
    keep_b, send_b, extra = backward_sums(x, hid, dback, dup, small)
    got_b = swap(send_b, "core")

    mine = reduce_all(keep_a, got_a, keep_b, got_b, extra, keep_sum, profile)
    other = swap(mine, "core")
    g_up, g_down, g_v, g_u, g_gu, g_gd, g_aw = unpack(other, *unpack(mine))
    return (
        pooled,
        g_up,
        g_down,
        g_gu.reshape(BOT),
        g_gd.reshape(FEAT),
        g_v,
        g_u,
        g_aw.reshape(ATT),
    )


def solution(mesh):
    fine = Mesh(mesh.devices.reshape(2, 4, 2, 8, 2), FINE)
    return jax.shard_map(
        per_device,
        mesh=fine,
        in_specs=(
            P(SLIDE, TILE, None, None),
            P(SLIDE, TILE),
            P(SLIDE, TILE),
            P(SLIDE, TILE),
            P(),
            P(),
            P(),
            P(),
            P(),
            P(),
            P(),
        ),
        out_specs=(P(SLIDE, None), P(), P(), P(), P(), P(), P(), P()),
        check_vma=False,
    )
```

```python
import functools

import jax
import jax.numpy as jnp
from jax import lax
from jax.experimental import pallas as pl
from jax.experimental.pallas import tpu as pltpu
from jax.sharding import Mesh
from jax.sharding import PartitionSpec as P

F32 = jnp.float32
BF16 = jnp.bfloat16

FINE = ("x_lo", "y", "x_hi", "z", "core")
SLIDE = ("x_lo", "y")
TILE = ("x_hi", "z", "core")
PLANE = ("x_lo", "y", "x_hi")
N_PLANE = 16
N_Z = 8

SLOTS = 32
POS = 64
FEAT = 1024
BOT = 256
ATT = 256
LANE = 128
STEPS = 4
GROUP = SLOTS // STEPS
PIECE = 32
HALF = 16
BLOCKS = FEAT // LANE
MAIN = PIECE * BLOCKS
TAIL = 32
TALL = MAIN + TAIL
SMALLS = 12
ROWS = GROUP * POS

CHUNKS = 8
CHUNK = SLOTS * POS // CHUNKS
LOADS = (512, 1536)

VMEM_LIMIT = 24 * 1024 * 1024
VMEM = pl.BlockSpec(memory_space=pltpu.VMEM)


def params():
    return pltpu.CompilerParams(vmem_limit_bytes=VMEM_LIMIT)


def nn(a, b):
    return jnp.dot(a, b, preferred_element_type=F32)


def nt(a, b):
    return lax.dot_general(a, b, (((1,), (1,)), ((), ())), preferred_element_type=F32)


def tn(a, b):
    return lax.dot_general(a, b, (((0,), (0,)), ((), ())), preferred_element_type=F32)


def sigmoid(v):
    return 1.0 / (1.0 + jnp.exp(-v))


def column(row):
    n = row.shape[1]
    i = lax.broadcasted_iota(jnp.int32, (n, n), 0)
    j = lax.broadcasted_iota(jnp.int32, (n, n), 1)
    return jnp.sum(jnp.where(i == j, jnp.broadcast_to(row, (n, n)), 0), axis=1, keepdims=True)


def members(ids_ref):
    ids = column(ids_ref[...])
    return [ids == c for c in range(4)], ids >= 0


def split3(v):
    hi = v.astype(BF16)
    rest = v - hi.astype(F32)
    mid = rest.astype(BF16)
    low = (rest - mid.astype(F32)).astype(BF16)
    return [hi, mid, low]


def slopes(tanh, sigm, aw):
    return aw * sigm * (1.0 - tanh * tanh), aw * tanh * sigm * (1.0 - sigm)


def forward_kernel(
    x_hbm, wu_hbm, wd_hbm, gu_hbm, gd_hbm, av_hbm, au_hbm, aw_hbm, ids_hbm, cot_hbm, count_ref,
    x_ref, hid_ref, up_ref, feat_ref, tanh_ref, sigm_ref, weight_ref, pack_ref, live_ref,
    wd_ref, gu_ref, gd_ref, av_ref, au_ref, aw_ref, wu_ref, ids_ref, cot_ref, sems,
):
    starts = [sum(LOADS[:i]) for i in range(len(LOADS))]
    loads = []
    for i, start in enumerate(starts):
        at = pl.ds(start, LOADS[i])
        loads.append(pltpu.make_async_copy(x_hbm.at[at, :], x_ref.at[at, :], sems.at[i]))
    pairs = [
        (wu_hbm, wu_ref),
        (gu_hbm, gu_ref),
        (wd_hbm, wd_ref),
        (gd_hbm, gd_ref),
        (av_hbm, av_ref),
        (au_hbm, au_ref),
        (aw_hbm, aw_ref),
        (ids_hbm, ids_ref),
        (cot_hbm, cot_ref),
    ]
    others = [
        pltpu.make_async_copy(src, dst, sems.at[len(LOADS) + i])
        for i, (src, dst) in enumerate(pairs)
    ]
    others[0].start()
    loads[0].start()
    for copy in others[1:4]:
        copy.start()
    for copy in loads[1:]:
        copy.start()
    for copy in others[4:]:
        copy.start()
    for copy in others[:4]:
        copy.wait()
    for i in range(CHUNKS):
        at = slice(i * CHUNK, (i + 1) * CHUNK)
        if i * CHUNK in starts:
            loads[starts.index(i * CHUNK)].wait()
        x = x_ref[at, :]
        up = nn(x, wu_ref[...])
        up_ref[at, :] = up
        hidden = jnp.maximum(up * gu_ref[...], 0.0).astype(BF16)
        hid_ref[at, :] = hidden
        down = nn(hidden, wd_ref[...])
        res = x.astype(F32) + down * gd_ref[...]
        feats = jnp.sum(jnp.maximum(res, 0.0).reshape(CHUNK // POS, POS, FEAT), axis=1)
        feat_ref[i * CHUNK // POS : (i + 1) * CHUNK // POS, :] = feats * (1.0 / POS)
    for copy in others[4:]:
        copy.wait()
    feat = feat_ref[...]
    feat_b = feat.astype(BF16)
    tanh = jnp.tanh(nn(feat_b, av_ref[...]))
    sigm = sigmoid(nn(feat_b, au_ref[...]))
    tanh_ref[...] = tanh
    sigm_ref[...] = sigm
    weight = sigmoid(jnp.sum(tanh * sigm * aw_ref[...], axis=1, keepdims=True))
    weight_ref[...] = jnp.broadcast_to(weight, (SLOTS, LANE))
    slot = lax.broadcasted_iota(jnp.int32, (1, SLOTS), 1)
    live_ref[...] = jnp.where(slot < count_ref[0, 0], ids_ref[...], -1)
    member, _ = members(live_ref)
    for c in range(4):
        share = jnp.where(member[c], weight, 0.0)
        num = jnp.sum(share * feat, axis=0, keepdims=True)
        den = jnp.sum(share, axis=0, keepdims=True)
        for r in range(8):
            pack_ref[8 * c + r : 8 * c + r + 1, :] = num[:, LANE * r : LANE * (r + 1)]
        pack_ref[36 + c : 37 + c, :] = jnp.broadcast_to(den, (1, LANE))
    quarter = lax.rem(lax.axis_index("z"), 2) * 2 + lax.axis_index("core")
    lane = lax.broadcasted_iota(jnp.int32, (4, LANE), 1)
    mine = jnp.logical_and(lane >= quarter * 32, lane < quarter * 32 + 32)
    cot = cot_ref[...].astype(F32)
    cot = jnp.concatenate([cot, cot, cot, cot], axis=1)
    pack_ref[32:36, :] = jnp.where(mine, cot, 0.0)


def keep_kernel(
    x_ref, hid_ref, wd_ref, gd_ref, tanh_ref, sigm_ref, aw_ref, av_ref, au_ref,
    mask_ref, act_ref, slope_ref,
):
    for i in range(CHUNKS):
        at = slice(i * CHUNK, (i + 1) * CHUNK)
        down = nn(hid_ref[at, :], wd_ref[...])
        positive = x_ref[at, :].astype(F32) + down * gd_ref[...] > 0
        mask_ref[at, :] = jnp.where(positive, 1.0, 0.0).astype(BF16)
        acts = jnp.where(positive, down, 0.0).reshape(CHUNK // POS, POS, FEAT)
        act_ref[i * CHUNK // POS : (i + 1) * CHUNK // POS, :] = jnp.sum(acts, axis=1)
    slope_t, slope_s = slopes(tanh_ref[...], sigm_ref[...], aw_ref[...])
    from_t = nt(jnp.concatenate(split3(slope_t), axis=0), av_ref[...])
    from_s = nt(jnp.concatenate(split3(slope_s), axis=0), au_ref[...])
    total = from_t[0:32] + from_t[32:64] + from_t[64:96]
    slope_ref[...] = total + (from_s[0:32] + from_s[32:64] + from_s[64:96])


def pair_kernel(mine_ref, other_ref, out_ref):
    out_ref[...] = mine_ref[...] + other_ref[...]


def spread_kernel(mine_ref, other_ref, out_ref):
    first = lax.axis_index("x_hi") == 0
    mine = mine_ref[...]
    other = other_ref[...]
    low = jnp.where(first, mine, other)[32:36]
    high = jnp.where(first, other, mine)[32:36]
    out = mine + other
    for p in range(N_Z):
        out_ref[p, 0:32, :] = out[0:32]
        out_ref[p, 32:36, :] = low + pltpu.roll(high, LANE // 2, 1)
        out_ref[p, 36:40, :] = out[36:40]


def middle_kernel(
    ids_ref, got_ref, feat_ref, act_ref, slope_ref, tanh_ref, sigm_ref, weight_ref,
    aw_ref, gd_ref,
    back_ref, pooled_ref, small_ref, keep_ref, send_ref, keep_sum_ref, profile_ref,
):
    core = lax.axis_index("core")
    total = got_ref[0]
    for p in range(1, N_Z):
        total = total + got_ref[p]
    even = lax.broadcasted_iota(jnp.int32, (4, LANE), 1) < LANE // 2
    cots = [got_ref[p, 32:36, :] for p in range(N_Z)]
    lows = [jnp.where(even, cots[p], cots[p + 1]) for p in range(0, N_Z, 2)]
    highs = [
        pltpu.roll(jnp.where(even, cots[p + 1], cots[p]), LANE // 2, 1) for p in range(0, N_Z, 2)
    ]
    cot = jnp.concatenate(lows + highs, axis=1)
    member, live = members(ids_ref)
    cot_tile = jnp.zeros((SLOTS, FEAT), F32)
    pooled_tile = jnp.zeros((SLOTS, FEAT), F32)
    den_tile = jnp.where(live, 0.0, 1.0)
    profile = jnp.zeros((1, FEAT), F32)
    for c in range(4):
        num = jnp.concatenate([total[8 * c + r : 8 * c + r + 1, :] for r in range(8)], axis=1)
        den = total[36 + c : 37 + c, 0:1]
        pooled = num / den
        pooled_ref[c : c + 1, :] = pooled
        profile = profile + pooled
        cot_tile = jnp.where(member[c], cot[c : c + 1, :], cot_tile)
        pooled_tile = jnp.where(member[c], pooled, pooled_tile)
        den_tile = jnp.where(member[c], den, den_tile)
    feat = feat_ref[...]
    tanh = tanh_ref[...]
    sigm = sigm_ref[...]
    weight = weight_ref[:, 0:1]
    aw = aw_ref[...]
    dweight = jnp.sum(cot_tile * (feat - pooled_tile), axis=1, keepdims=True) / den_tile
    dscore = dweight * weight * (1.0 - weight)
    grad_aw = jnp.sum(dscore * tanh * sigm, axis=0, keepdims=True)
    slope_t, slope_s = slopes(tanh, sigm, aw)
    grad_t = dscore * slope_t
    grad_s = dscore * slope_s
    profile = (profile * 0.25).astype(BF16).astype(F32)
    norm = jnp.maximum(jnp.sum(profile * profile, axis=1, keepdims=True), 1e-30)
    feat_b = feat.astype(BF16).astype(F32)
    along = jnp.sum(feat_b * profile, axis=1, keepdims=True) / norm
    rest = feat_b - along * profile
    rest_0, rest_1, _ = split3(rest)
    rest_3 = jnp.concatenate([rest_0, rest_0, rest_1], axis=0)
    grad_t0, grad_t1, _ = split3(grad_t)
    grad_s0, grad_s1, _ = split3(grad_s)
    grad_v = tn(jnp.concatenate([grad_t0, grad_t1, grad_t0], axis=0), rest_3)
    grad_u = tn(jnp.concatenate([grad_s0, grad_s1, grad_s0], axis=0), rest_3)
    sum_t = jnp.sum(along * grad_t, axis=0, keepdims=True)
    sum_s = jnp.sum(along * grad_s, axis=0, keepdims=True)
    for r in range(8):
        profile_ref[r : r + 1, :] = profile[:, LANE * r : LANE * (r + 1)]
    keep_sum_ref[...] = jnp.where(core == 0, sum_t, sum_s)
    sent = jnp.where(core == 0, sum_s, sum_t)
    high = sent.astype(BF16)
    send_ref[ATT : ATT + HALF, :] = jnp.zeros((HALF, FEAT), BF16)
    send_ref[ATT : ATT + HALF, 0:ATT] = jnp.broadcast_to(high, (HALF, ATT))
    low = (sent - high.astype(F32)).astype(BF16)
    send_ref[ATT : ATT + HALF, ATT : 2 * ATT] = jnp.broadcast_to(low, (HALF, ATT))

    @pl.when(core == 0)
    def _():
        keep_ref[...] = grad_v
        send_ref[0:ATT, :] = grad_u.astype(BF16)

    @pl.when(core != 0)
    def _():
        keep_ref[...] = grad_u
        send_ref[0:ATT, :] = grad_v.astype(BF16)

    dfeat = ((weight / den_tile) * cot_tile + dscore * slope_ref[...]) * (1.0 / POS)
    back_ref[...] = (dfeat * gd_ref[...]).astype(BF16).astype(F32)
    grad_gd = jnp.sum(dfeat * act_ref[...], axis=0, keepdims=True)
    for r in range(8):
        small_ref[r : r + 1, :] = grad_gd[:, LANE * r : LANE * (r + 1)]
    for r in range(2):
        small_ref[8 + r : 9 + r, :] = grad_aw[:, LANE * r : LANE * (r + 1)]
    small_ref[10:16, :] = jnp.zeros((6, LANE), F32)


def rows_kernel(
    mask_ref, up_ref, back_ref, small_ref, wd_ref, gu_ref, dback_ref, dup_ref, out_ref
):
    gu = gu_ref[...]
    gain = jnp.zeros((8, BOT), F32)
    for i in range(STEPS):
        at = slice(ROWS * i, ROWS * (i + 1))
        for k in range(GROUP):
            tile = GROUP * i + k
            row = back_ref[tile : tile + 1, :].astype(BF16)
            here = slice(POS * tile, POS * (tile + 1))
            dback_ref[here, :] = mask_ref[here, :] * jnp.broadcast_to(row, (POS, FEAT))
        dhid = nt(dback_ref[at, :], wd_ref[...])
        up = up_ref[at, :]
        dscaled = jnp.where(up * gu > 0, dhid, 0.0)
        gain = gain + jnp.sum((dscaled * up).reshape(ROWS // 8, 8, BOT), axis=0)
        dup_ref[at, :] = (dscaled * gu).astype(BF16)
    gain = jnp.sum(gain, axis=0, keepdims=True)
    out_ref[0:10, :] = small_ref[0:10, :]
    out_ref[10:11, :] = gain[:, 0:LANE]
    out_ref[11:12, :] = gain[:, LANE : 2 * LANE]
    out_ref[12:HALF, :] = jnp.zeros((HALF - 12, LANE), F32)


def sums_kernel(x_ref, hid_ref, dback_ref, dup_ref, small_ref, keep_ref, send_ref, extra_ref):
    small = small_ref[...]
    first = lax.axis_index("core") == 0
    down = tn(hid_ref[...], dback_ref[...])
    up_grad = tn(dup_ref[...], x_ref[...])

    @pl.when(first)
    def _():
        keep_ref[...] = down
        extra_ref[...] = small
        send_ref[0:BOT, :] = up_grad.astype(BF16)

    @pl.when(jnp.logical_not(first))
    def _():
        keep_ref[...] = up_grad
        extra_ref[...] = jnp.zeros((HALF, LANE), F32)
        send_ref[0:BOT, :] = down.astype(BF16)

    sent = jnp.where(first, 0.0, small)
    high = sent.astype(BF16)
    send_ref[BOT : BOT + HALF, :] = jnp.zeros((HALF, FEAT), BF16)
    send_ref[BOT : BOT + HALF, 0:LANE] = high
    send_ref[BOT : BOT + HALF, LANE : 2 * LANE] = (sent - high.astype(F32)).astype(BF16)


def paired_kernel(
    keep_a_ref, got_a_ref, keep_b_ref, got_b_ref, extra_ref, keep_sum_ref, out_ref, sum_ref
):
    total = keep_sum_ref[...]
    for start in (0, ATT):
        term = got_a_ref[ATT : ATT + HALF, start : start + ATT].astype(F32)
        total = total + term[0:1, :]
    sum_ref[0:1, :] = total[:, 0:LANE]
    sum_ref[1:2, :] = total[:, LANE : 2 * LANE]
    sum_ref[14:16, :] = jnp.zeros((2, LANE), F32)
    for p in range(N_PLANE):
        at = slice(HALF * p, HALF * (p + 1))
        for j in range(BLOCKS):
            lanes = slice(LANE * j, LANE * (j + 1))
            sum_a = keep_a_ref[at, lanes] + got_a_ref[at, lanes].astype(F32)
            sum_b = keep_b_ref[at, lanes] + got_b_ref[at, lanes].astype(F32)
            out_ref[p, PIECE * j : PIECE * j + HALF, :] = sum_a.astype(BF16)
            out_ref[p, PIECE * j + HALF : PIECE * (j + 1), :] = sum_b.astype(BF16)
    small = extra_ref[0:SMALLS, :]
    for col in (slice(0, LANE), slice(LANE, 2 * LANE)):
        small = small + got_b_ref[BOT : BOT + HALF, col].astype(F32)[0:SMALLS, :]
    sum_ref[2 : 2 + SMALLS, :] = small


def tail_parts(ref):
    tail = ref[MAIN:TALL, :].astype(F32)
    return tail[0:4], tail[4:6] + tail[6:8], tail[8:20] + tail[20:32]


def tail_block(profile, sums, small):
    sums_high = sums.astype(BF16).astype(F32)
    high = small.astype(BF16).astype(F32)
    rows = [profile, sums_high, sums - sums_high, high, small - high]
    return jnp.concatenate(rows, axis=0).astype(BF16)


def plane_sum_kernel(got_ref, profile_ref, sum_ref, out_ref):
    total = got_ref[0].astype(F32)
    for p in range(1, N_PLANE):
        total = total + got_ref[p].astype(F32)
    out_ref[0:MAIN, :] = total.astype(BF16)
    profile = profile_ref[...]
    profile = jnp.where(lax.axis_index("x_hi") == 0, profile[0:4], profile[4:8])
    out_ref[MAIN:TALL, :] = tail_block(profile, sum_ref[0:2, :], sum_ref[2 : 2 + SMALLS, :])


def z_pair_kernel(mine_ref, other_ref, out_ref):
    total = mine_ref[0:MAIN, :].astype(F32) + other_ref[0:MAIN, :].astype(F32)
    out_ref[0:MAIN, :] = total.astype(BF16)
    profile, sums, small = tail_parts(mine_ref)
    _, sums_o, small_o = tail_parts(other_ref)
    out_ref[MAIN:TALL, :] = tail_block(profile, sums + sums_o, small + small_o)


def z_sum_kernel(mine_ref, near_ref, cross_ref, far_ref, out_ref):
    near = mine_ref[0:MAIN, :].astype(F32) + near_ref[0:MAIN, :].astype(F32)
    far = far_ref[0:MAIN, :].astype(F32) + cross_ref[0:MAIN, :].astype(F32)
    main = (near + far).astype(BF16)
    profile, sums, small = tail_parts(mine_ref)
    _, sums_n, small_n = tail_parts(near_ref)
    _, sums_f, small_f = tail_parts(far_ref)
    _, sums_c, small_c = tail_parts(cross_ref)
    sums = (sums + sums_n) + (sums_f + sums_c)
    tail = tail_block(profile, sums, (small + small_n) + (small_f + small_c))
    for p in range(N_PLANE):
        out_ref[p, 0:MAIN, :] = main
        out_ref[p, MAIN:TALL, :] = tail


def unpack_kernel(own, got_ref, *refs):
    up_hbm, down_hbm, v_hbm, u_hbm, gup_hbm, gdown_hbm, aw_hbm = refs[-14:-7]
    attn_ref, down_ref, up_ref, gup_ref, gdown_ref, aw_ref, sems = refs[-7:]
    first = (lax.axis_index("core") == 0) if own else (lax.axis_index("core") != 0)

    def halves(src, dst, sem):
        rows = src.shape[0] // 2
        cuts = [pl.ds(rows * h, rows) for h in range(2)]
        return [
            pltpu.make_async_copy(src.at[cut, :], dst.at[cut, :], sems.at[sem + h])
            for h, cut in enumerate(cuts)
        ]

    to_v = halves(attn_ref, v_hbm, 0)
    to_u = halves(attn_ref, u_hbm, 0)
    to_down = halves(down_ref, down_hbm, 2)
    to_up = halves(up_ref, up_hbm, 2)
    smalls = [
        pltpu.make_async_copy(gup_ref, gup_hbm, sems.at[4]),
        pltpu.make_async_copy(gdown_ref, gdown_hbm, sems.at[5]),
        pltpu.make_async_copy(aw_ref, aw_hbm, sems.at[6]),
    ]
    tails = [got_ref[p, MAIN:TALL, :].astype(F32) for p in range(N_PLANE)]
    sums = [tail[4:6] + tail[6:8] for tail in tails]
    sums = [sums[p] + sums[p + 1] for p in range(0, N_PLANE, 2)]
    sums = [jnp.concatenate([v[0:1], v[1:2]], axis=1) for v in sums]
    sums = jnp.concatenate(split3(jnp.concatenate(sums, axis=0)), axis=0)
    for j in range(BLOCKS):
        rows = slice(PIECE * j, PIECE * j + HALF)
        attn = got_ref[:, rows, :].astype(F32).reshape(ATT, LANE)
        row = slice(j % 4, j % 4 + 1)
        profile = [tails[p + j // 4][row] for p in range(0, N_PLANE, 2)]
        profile = jnp.concatenate([v for _ in range(3) for v in profile], axis=0)
        outer = tn(profile.astype(BF16), sums)
        attn_ref[LANE * j : LANE * (j + 1), :] = attn.T + outer
        if j % 4 == 3:

            @pl.when(first)
            def _():
                to_v[j // 4].start()

            @pl.when(jnp.logical_not(first))
            def _():
                to_u[j // 4].start()

    @pl.when(first)
    def _():
        for h in range(2):
            pieces = slice(N_PLANE // 2 * h, N_PLANE // 2 * (h + 1))
            at = slice(BOT // 2 * h, BOT // 2 * (h + 1))
            for j in range(BLOCKS):
                rows = slice(PIECE * j + HALF, PIECE * (j + 1))
                enc = got_ref[pieces, rows, :].astype(F32).reshape(BOT // 2, LANE)
                down_ref[at, LANE * j : LANE * (j + 1)] = enc
            to_down[h].start()
        small = tails[0][8:20] + tails[0][20:32]
        for tail in tails[1:]:
            small = small + (tail[8:20] + tail[20:32])
        for r in range(SMALLS):
            if r < 8:
                gdown_ref[:, LANE * r : LANE * (r + 1)] = small[r : r + 1]
            elif r < 10:
                aw_ref[:, LANE * (r - 8) : LANE * (r - 7)] = small[r : r + 1]
            else:
                gup_ref[:, LANE * (r - 10) : LANE * (r - 9)] = small[r : r + 1]
        for copy in smalls:
            copy.start()
        for copy in to_v + to_down + smalls:
            copy.wait()

    @pl.when(jnp.logical_not(first))
    def _():
        for h in range(2):
            for j in range(4 * h, 4 * h + 4):
                rows = slice(PIECE * j + HALF, PIECE * (j + 1))
                enc = got_ref[:, rows, :].astype(F32).reshape(BOT, LANE)
                up_ref[LANE * j : LANE * (j + 1), :] = enc.T
            to_up[h].start()
        for copy in to_u + to_up:
            copy.wait()


def whole_spec(shape):
    return pl.BlockSpec(shape, lambda *_: (0,) * len(shape))


def call(body, outs, *args, name):
    return pl.pallas_call(
        body,
        out_shape=[jax.ShapeDtypeStruct(s, d) for s, d in outs],
        compiler_params=params(),
        name=name,
    )(*args)


def swap(v, axis):
    return lax.ppermute(v, axis, [(0, 1), (1, 0)])


def in_hbm(*arrays):
    return [pltpu.with_memory_space_constraint(v, pltpu.HBM) for v in arrays]


def reduce_all(keep_a, got_a, keep_b, got_b, extra, keep_sum, profile):
    pieces = (N_PLANE, TALL, LANE)
    scattered = (N_PLANE, MAIN, LANE)
    paired, sums = call(
        paired_kernel,
        [(scattered, BF16), ((HALF, LANE), F32)],
        keep_a, got_a, keep_b, got_b, extra, keep_sum,
        name="paired",
    )
    got = lax.all_to_all(paired, PLANE, 0, 0, tiled=True)
    flat = [(pieces[1:], BF16)]
    (part,) = call(plane_sum_kernel, flat, got, profile, sums, name="plane_sum")
    (pair,) = call(z_pair_kernel, flat, part, cross_z(part, 1), name="z_pair")
    near, cross, far = [cross_z(pair, bits) for bits in (2, 6, 4)]
    (whole,) = call(
        z_sum_kernel,
        [(pieces, BF16)],
        pair, near, cross, far,
        name="z_sum",
    )
    return lax.all_to_all(whole, PLANE, 0, 0, tiled=True)


def cross_z(v, bits):
    return lax.ppermute(v, "z", [(i, i ^ bits) for i in range(N_Z)])


def unpack(got, *before):
    hbm = pl.BlockSpec(memory_space=pltpu.HBM)
    shapes = [
        (FEAT, BOT), (BOT, FEAT), (FEAT, ATT), (FEAT, ATT), (1, BOT), (1, FEAT), (1, ATT)
    ]
    return pl.pallas_call(
        functools.partial(unpack_kernel, not before),
        in_specs=[VMEM] + [hbm] * len(before),
        out_specs=[hbm] * len(shapes),
        out_shape=[jax.ShapeDtypeStruct(v, F32) for v in shapes],
        input_output_aliases={1 + i: i for i in range(len(before))},
        scratch_shapes=[
            pltpu.VMEM((FEAT, ATT), F32),
            pltpu.VMEM((BOT, FEAT), F32),
            pltpu.VMEM((FEAT, BOT), F32),
            pltpu.VMEM((1, BOT), F32),
            pltpu.VMEM((1, FEAT), F32),
            pltpu.VMEM((1, ATT), F32),
            pltpu.SemaphoreType.DMA((7,)),
        ],
        compiler_params=params(),
        name="unpack_other" if before else "unpack_own",
    )(got, *before)


def encode(
    rows, slide_ids, counts, pooled_cot, w_up, w_down, gu, gd, attn_v, attn_u, aw
):
    hbm = pl.BlockSpec(memory_space=pltpu.HBM)
    outs = [
        ((SLOTS * POS, FEAT), BF16),
        ((SLOTS * POS, BOT), BF16),
        ((SLOTS * POS, BOT), F32),
        ((SLOTS, FEAT), F32),
        ((SLOTS, ATT), F32),
        ((SLOTS, ATT), F32),
        ((SLOTS, LANE), F32),
        ((40, LANE), F32),
        ((1, SLOTS), jnp.int32),
        ((BOT, FEAT), BF16),
        ((1, BOT), F32),
        ((1, FEAT), F32),
        ((FEAT, ATT), BF16),
        ((FEAT, ATT), BF16),
        ((1, ATT), F32),
    ]
    return pl.pallas_call(
        forward_kernel,
        in_specs=[hbm] * 10 + [pl.BlockSpec(memory_space=pltpu.SMEM)],
        out_specs=[VMEM] * len(outs),
        out_shape=[jax.ShapeDtypeStruct(s, d) for s, d in outs],
        scratch_shapes=[
            pltpu.VMEM((FEAT, BOT), BF16),
            pltpu.VMEM((1, SLOTS), jnp.int32),
            pltpu.VMEM((4, 32), BF16),
            pltpu.SemaphoreType.DMA((len(LOADS) + 9,)),
        ],
        compiler_params=params(),
        name="encode",
    )(*in_hbm(rows, w_up, w_down, gu, gd, attn_v, attn_u, aw, slide_ids, pooled_cot), counts)


def backward_rows(mask, up, back, small, w_down, gu):
    outs = [((SLOTS * POS, FEAT), BF16), ((SLOTS * POS, BOT), BF16), ((HALF, LANE), F32)]
    return call(rows_kernel, outs, mask, up, back, small, w_down, gu, name="backward_rows")


def backward_sums(x, hid, dback, dup, small):
    outs = [((BOT, FEAT), F32), ((BOT + HALF, FEAT), BF16), ((HALF, LANE), F32)]
    return call(sums_kernel, outs, x, hid, dback, dup, small, name="backward_sums")


def per_device(
    tiles, counts, slide_ids, pooled_cot, w_up, w_down, gain_up, gain_down, attn_v, attn_u, attn_w
):
    rows = tiles.reshape(SLOTS * POS, FEAT)
    gu = gain_up.reshape(1, BOT)
    gd = gain_down.reshape(1, FEAT)
    aw = attn_w.reshape(1, ATT)
    x, hid, up, feat, tanh, sigm, weight, pack, ids, *loaded = encode(
        rows, slide_ids, counts, pooled_cot, w_up, w_down, gu, gd, attn_v, attn_u, aw
    )
    w_down, gu, gd, attn_v, attn_u, aw = loaded
    (half,) = call(pair_kernel, [((40, LANE), F32)], pack, swap(pack, "core"), name="pair")
    mask, act, slope = call(
        keep_kernel,
        [((SLOTS * POS, FEAT), BF16), ((SLOTS, FEAT), F32), ((SLOTS, FEAT), F32)],
        x, hid, w_down, gd, tanh, sigm, aw, attn_v, attn_u,
        name="keep",
    )
    across, mask, act, slope = lax.optimization_barrier((swap(half, "x_hi"), mask, act, slope))
    (spread,) = call(spread_kernel, [((N_Z, 40, LANE), F32)], half, across, name="spread")
    got = lax.all_to_all(spread, "z", 0, 0, tiled=True)

    back, pooled, small, keep_a, send_a, keep_sum, profile = pl.pallas_call(
        middle_kernel,
        in_specs=[VMEM] * 10,
        out_shape=[
            jax.ShapeDtypeStruct((SLOTS, FEAT), F32),
            jax.ShapeDtypeStruct((4, FEAT), F32),
            jax.ShapeDtypeStruct((16, LANE), F32),
            jax.ShapeDtypeStruct((ATT, FEAT), F32),
            jax.ShapeDtypeStruct((ATT + HALF, FEAT), BF16),
            jax.ShapeDtypeStruct((1, ATT), F32),
            jax.ShapeDtypeStruct((8, LANE), F32),
        ],
        compiler_params=params(),
        name="middle",
    )(ids, got, feat, act, slope, tanh, sigm, weight, aw, gd)

    dback, dup, small = backward_rows(mask, up, back, small, w_down, gu)
    got_a, dback = lax.optimization_barrier((swap(send_a, "core"), dback))
    keep_b, send_b, extra = backward_sums(x, hid, dback, dup, small)
    got_b = swap(send_b, "core")

    mine = reduce_all(keep_a, got_a, keep_b, got_b, extra, keep_sum, profile)
    other = swap(mine, "core")
    g_up, g_down, g_v, g_u, g_gu, g_gd, g_aw = unpack(other, *unpack(mine))
    return (
        pooled,
        g_up,
        g_down,
        g_gu.reshape(BOT),
        g_gd.reshape(FEAT),
        g_v,
        g_u,
        g_aw.reshape(ATT),
    )


def solution(mesh):
    fine = Mesh(mesh.devices.reshape(2, 4, 2, 8, 2), FINE)
    return jax.shard_map(
        per_device,
        mesh=fine,
        in_specs=(
            P(SLIDE, TILE, None, None),
            P(SLIDE, TILE),
            P(SLIDE, TILE),
            P(SLIDE, TILE),
            P(),
            P(),
            P(),
            P(),
            P(),
            P(),
            P(),
        ),
        out_specs=(P(SLIDE, None), P(), P(), P(), P(), P(), P(), P()),
        check_vma=False,
    )
```

```python
import functools

import jax
import jax.numpy as jnp
from jax import lax
from jax.experimental import pallas as pl
from jax.experimental.pallas import tpu as pltpu
from jax.sharding import Mesh
from jax.sharding import PartitionSpec as P

F32 = jnp.float32
BF16 = jnp.bfloat16

FINE = ("x_lo", "y", "x_hi", "z", "core")
SLIDE = ("x_lo", "y")
TILE = ("x_hi", "z", "core")
PLANE = ("x_lo", "y", "x_hi")
N_PLANE = 16
N_Z = 8

SLOTS = 32
POS = 64
FEAT = 1024
BOT = 256
ATT = 256
LANE = 128
STEPS = 4
GROUP = SLOTS // STEPS
PIECE = 32
HALF = 16
BLOCKS = FEAT // LANE
MAIN = PIECE * BLOCKS
TALL = MAIN + HALF
ROWS = GROUP * POS

CHUNKS = 8
CHUNK = SLOTS * POS // CHUNKS
LOADS = (512, 1536)

VMEM_LIMIT = 24 * 1024 * 1024
VMEM = pl.BlockSpec(memory_space=pltpu.VMEM)


def params():
    return pltpu.CompilerParams(vmem_limit_bytes=VMEM_LIMIT)


def nn(a, b):
    return jnp.dot(a, b, preferred_element_type=F32)


def nt(a, b):
    return lax.dot_general(a, b, (((1,), (1,)), ((), ())), preferred_element_type=F32)


def tn(a, b):
    return lax.dot_general(a, b, (((0,), (0,)), ((), ())), preferred_element_type=F32)


def sigmoid(v):
    return 1.0 / (1.0 + jnp.exp(-v))


def column(row):
    n = row.shape[1]
    i = lax.broadcasted_iota(jnp.int32, (n, n), 0)
    j = lax.broadcasted_iota(jnp.int32, (n, n), 1)
    return jnp.sum(jnp.where(i == j, jnp.broadcast_to(row, (n, n)), 0), axis=1, keepdims=True)


def members(ids_ref):
    ids = column(ids_ref[...])
    return [ids == c for c in range(4)], ids >= 0


def split3(v):
    hi = v.astype(BF16)
    rest = v - hi.astype(F32)
    mid = rest.astype(BF16)
    low = (rest - mid.astype(F32)).astype(BF16)
    return [hi, mid, low]


def slopes(tanh, sigm, aw):
    return aw * sigm * (1.0 - tanh * tanh), aw * tanh * sigm * (1.0 - sigm)


def forward_kernel(
    x_hbm, wu_hbm, wd_hbm, gu_hbm, gd_hbm, av_hbm, au_hbm, aw_hbm, ids_hbm, cot_hbm, count_ref,
    x_ref, hid_ref, up_ref, feat_ref, tanh_ref, sigm_ref, weight_ref, pack_ref, live_ref,
    wd_ref, gu_ref, gd_ref, av_ref, au_ref, aw_ref, wu_ref, ids_ref, cot_ref, sems,
):
    starts = [sum(LOADS[:i]) for i in range(len(LOADS))]
    loads = []
    for i, start in enumerate(starts):
        at = pl.ds(start, LOADS[i])
        loads.append(pltpu.make_async_copy(x_hbm.at[at, :], x_ref.at[at, :], sems.at[i]))
    pairs = [
        (wu_hbm, wu_ref),
        (gu_hbm, gu_ref),
        (wd_hbm, wd_ref),
        (gd_hbm, gd_ref),
        (av_hbm, av_ref),
        (au_hbm, au_ref),
        (aw_hbm, aw_ref),
        (ids_hbm, ids_ref),
        (cot_hbm, cot_ref),
    ]
    others = [
        pltpu.make_async_copy(src, dst, sems.at[len(LOADS) + i])
        for i, (src, dst) in enumerate(pairs)
    ]
    others[0].start()
    loads[0].start()
    for copy in others[1:4]:
        copy.start()
    for copy in loads[1:]:
        copy.start()
    for copy in others[4:]:
        copy.start()
    for copy in others[:4]:
        copy.wait()
    for i in range(CHUNKS):
        at = slice(i * CHUNK, (i + 1) * CHUNK)
        if i * CHUNK in starts:
            loads[starts.index(i * CHUNK)].wait()
        x = x_ref[at, :]
        up = nn(x, wu_ref[...])
        up_ref[at, :] = up
        hidden = jnp.maximum(up * gu_ref[...], 0.0).astype(BF16)
        hid_ref[at, :] = hidden
        down = nn(hidden, wd_ref[...])
        res = x.astype(F32) + down * gd_ref[...]
        feats = jnp.sum(jnp.maximum(res, 0.0).reshape(CHUNK // POS, POS, FEAT), axis=1)
        feat_ref[i * CHUNK // POS : (i + 1) * CHUNK // POS, :] = feats * (1.0 / POS)
    for copy in others[4:]:
        copy.wait()
    feat = feat_ref[...]
    feat_b = feat.astype(BF16)
    tanh = jnp.tanh(nn(feat_b, av_ref[...]))
    sigm = sigmoid(nn(feat_b, au_ref[...]))
    tanh_ref[...] = tanh
    sigm_ref[...] = sigm
    weight = sigmoid(jnp.sum(tanh * sigm * aw_ref[...], axis=1, keepdims=True))
    weight_ref[...] = jnp.broadcast_to(weight, (SLOTS, LANE))
    slot = lax.broadcasted_iota(jnp.int32, (1, SLOTS), 1)
    live_ref[...] = jnp.where(slot < count_ref[0, 0], ids_ref[...], -1)
    member, _ = members(live_ref)
    for c in range(4):
        share = jnp.where(member[c], weight, 0.0)
        num = jnp.sum(share * feat, axis=0, keepdims=True)
        den = jnp.sum(share, axis=0, keepdims=True)
        for r in range(8):
            pack_ref[8 * c + r : 8 * c + r + 1, :] = num[:, LANE * r : LANE * (r + 1)]
        pack_ref[36 + c : 37 + c, :] = jnp.broadcast_to(den, (1, LANE))
    quarter = lax.rem(lax.axis_index("z"), 2) * 2 + lax.axis_index("core")
    lane = lax.broadcasted_iota(jnp.int32, (4, LANE), 1)
    mine = jnp.logical_and(lane >= quarter * 32, lane < quarter * 32 + 32)
    cot = cot_ref[...].astype(F32)
    cot = jnp.concatenate([cot, cot, cot, cot], axis=1)
    pack_ref[32:36, :] = jnp.where(mine, cot, 0.0)


def keep_kernel(
    x_ref, hid_ref, wd_ref, gd_ref, tanh_ref, sigm_ref, aw_ref, av_ref, au_ref,
    mask_ref, act_ref, slope_ref,
):
    for i in range(CHUNKS):
        at = slice(i * CHUNK, (i + 1) * CHUNK)
        down = nn(hid_ref[at, :], wd_ref[...])
        positive = x_ref[at, :].astype(F32) + down * gd_ref[...] > 0
        mask_ref[at, :] = jnp.where(positive, 1.0, 0.0).astype(BF16)
        acts = jnp.where(positive, down, 0.0).reshape(CHUNK // POS, POS, FEAT)
        act_ref[i * CHUNK // POS : (i + 1) * CHUNK // POS, :] = jnp.sum(acts, axis=1)
    slope_t, slope_s = slopes(tanh_ref[...], sigm_ref[...], aw_ref[...])
    from_t = nt(jnp.concatenate(split3(slope_t), axis=0), av_ref[...])
    from_s = nt(jnp.concatenate(split3(slope_s), axis=0), au_ref[...])
    total = from_t[0:32] + from_t[32:64] + from_t[64:96]
    slope_ref[...] = total + (from_s[0:32] + from_s[32:64] + from_s[64:96])


def pair_kernel(mine_ref, other_ref, out_ref):
    out_ref[...] = mine_ref[...] + other_ref[...]


def spread_kernel(mine_ref, other_ref, out_ref):
    first = lax.axis_index("x_hi") == 0
    mine = mine_ref[...]
    other = other_ref[...]
    low = jnp.where(first, mine, other)[32:36]
    high = jnp.where(first, other, mine)[32:36]
    out = mine + other
    for p in range(N_Z):
        out_ref[p, 0:32, :] = out[0:32]
        out_ref[p, 32:36, :] = low + pltpu.roll(high, LANE // 2, 1)
        out_ref[p, 36:40, :] = out[36:40]


def middle_kernel(
    ids_ref, got_ref, feat_ref, act_ref, slope_ref, tanh_ref, sigm_ref, weight_ref,
    aw_ref, gd_ref,
    back_ref, pooled_ref, small_ref, keep_ref, send_ref, keep_sum_ref, profile_ref,
):
    core = lax.axis_index("core")
    total = got_ref[0]
    for p in range(1, N_Z):
        total = total + got_ref[p]
    even = lax.broadcasted_iota(jnp.int32, (4, LANE), 1) < LANE // 2
    cots = [got_ref[p, 32:36, :] for p in range(N_Z)]
    lows = [jnp.where(even, cots[p], cots[p + 1]) for p in range(0, N_Z, 2)]
    highs = [
        pltpu.roll(jnp.where(even, cots[p + 1], cots[p]), LANE // 2, 1) for p in range(0, N_Z, 2)
    ]
    cot = jnp.concatenate(lows + highs, axis=1)
    member, live = members(ids_ref)
    cot_tile = jnp.zeros((SLOTS, FEAT), F32)
    pooled_tile = jnp.zeros((SLOTS, FEAT), F32)
    den_tile = jnp.where(live, 0.0, 1.0)
    profile = jnp.zeros((1, FEAT), F32)
    for c in range(4):
        num = jnp.concatenate([total[8 * c + r : 8 * c + r + 1, :] for r in range(8)], axis=1)
        den = total[36 + c : 37 + c, 0:1]
        pooled = num / den
        pooled_ref[c : c + 1, :] = pooled
        profile = profile + pooled
        cot_tile = jnp.where(member[c], cot[c : c + 1, :], cot_tile)
        pooled_tile = jnp.where(member[c], pooled, pooled_tile)
        den_tile = jnp.where(member[c], den, den_tile)
    feat = feat_ref[...]
    tanh = tanh_ref[...]
    sigm = sigm_ref[...]
    weight = weight_ref[:, 0:1]
    aw = aw_ref[...]
    dweight = jnp.sum(cot_tile * (feat - pooled_tile), axis=1, keepdims=True) / den_tile
    dscore = dweight * weight * (1.0 - weight)
    grad_aw = jnp.sum(dscore * tanh * sigm, axis=0, keepdims=True)
    slope_t, slope_s = slopes(tanh, sigm, aw)
    grad_t = dscore * slope_t
    grad_s = dscore * slope_s
    profile = (profile * 0.25).astype(BF16).astype(F32)
    norm = jnp.maximum(jnp.sum(profile * profile, axis=1, keepdims=True), 1e-30)
    feat_b = feat.astype(BF16).astype(F32)
    along = jnp.sum(feat_b * profile, axis=1, keepdims=True) / norm
    rest = feat_b - along * profile
    rest_0, rest_1, _ = split3(rest)
    rest_3 = jnp.concatenate([rest_0, rest_0, rest_1], axis=0)
    grad_t0, grad_t1, _ = split3(grad_t)
    grad_s0, grad_s1, _ = split3(grad_s)
    grad_v = tn(jnp.concatenate([grad_t0, grad_t1, grad_t0], axis=0), rest_3)
    grad_u = tn(jnp.concatenate([grad_s0, grad_s1, grad_s0], axis=0), rest_3)
    sum_t = jnp.sum(along * grad_t, axis=0, keepdims=True)
    sum_s = jnp.sum(along * grad_s, axis=0, keepdims=True)
    for r in range(8):
        profile_ref[r : r + 1, :] = profile[:, LANE * r : LANE * (r + 1)]
    keep_sum_ref[...] = jnp.where(core == 0, sum_t, sum_s)
    sent = jnp.where(core == 0, sum_s, sum_t)
    high = sent.astype(BF16)
    send_ref[ATT : ATT + HALF, :] = jnp.zeros((HALF, FEAT), BF16)
    send_ref[ATT : ATT + HALF, 0:ATT] = jnp.broadcast_to(high, (HALF, ATT))
    low = (sent - high.astype(F32)).astype(BF16)
    send_ref[ATT : ATT + HALF, ATT : 2 * ATT] = jnp.broadcast_to(low, (HALF, ATT))

    @pl.when(core == 0)
    def _():
        keep_ref[...] = grad_v
        send_ref[0:ATT, :] = grad_u.astype(BF16)

    @pl.when(core != 0)
    def _():
        keep_ref[...] = grad_u
        send_ref[0:ATT, :] = grad_v.astype(BF16)

    dfeat = ((weight / den_tile) * cot_tile + dscore * slope_ref[...]) * (1.0 / POS)
    back_ref[...] = (dfeat * gd_ref[...]).astype(BF16).astype(F32)
    grad_gd = jnp.sum(dfeat * act_ref[...], axis=0, keepdims=True)
    for r in range(8):
        small_ref[r : r + 1, :] = grad_gd[:, LANE * r : LANE * (r + 1)]
    for r in range(2):
        small_ref[8 + r : 9 + r, :] = grad_aw[:, LANE * r : LANE * (r + 1)]
    small_ref[10:16, :] = jnp.zeros((6, LANE), F32)


def rows_kernel(
    mask_ref, up_ref, back_ref, small_ref, wd_ref, gu_ref, dback_ref, dup_ref, out_ref
):
    gu = gu_ref[...]
    gain = jnp.zeros((8, BOT), F32)
    for i in range(STEPS):
        at = slice(ROWS * i, ROWS * (i + 1))
        for k in range(GROUP):
            tile = GROUP * i + k
            row = back_ref[tile : tile + 1, :].astype(BF16)
            here = slice(POS * tile, POS * (tile + 1))
            dback_ref[here, :] = mask_ref[here, :] * jnp.broadcast_to(row, (POS, FEAT))
        dhid = nt(dback_ref[at, :], wd_ref[...])
        up = up_ref[at, :]
        dscaled = jnp.where(up * gu > 0, dhid, 0.0)
        gain = gain + jnp.sum((dscaled * up).reshape(ROWS // 8, 8, BOT), axis=0)
        dup_ref[at, :] = (dscaled * gu).astype(BF16)
    gain = jnp.sum(gain, axis=0, keepdims=True)
    out_ref[0:10, :] = small_ref[0:10, :]
    out_ref[10:11, :] = gain[:, 0:LANE]
    out_ref[11:12, :] = gain[:, LANE : 2 * LANE]
    out_ref[12:HALF, :] = jnp.zeros((HALF - 12, LANE), F32)


def sums_kernel(x_ref, hid_ref, dback_ref, dup_ref, small_ref, keep_ref, send_ref, extra_ref):
    small = small_ref[...]
    first = lax.axis_index("core") == 0
    down = tn(hid_ref[...], dback_ref[...])
    up_grad = tn(dup_ref[...], x_ref[...])

    @pl.when(first)
    def _():
        keep_ref[...] = down
        extra_ref[...] = small
        send_ref[0:BOT, :] = up_grad.astype(BF16)

    @pl.when(jnp.logical_not(first))
    def _():
        keep_ref[...] = up_grad
        extra_ref[...] = jnp.zeros((HALF, LANE), F32)
        send_ref[0:BOT, :] = down.astype(BF16)

    sent = jnp.where(first, 0.0, small)
    high = sent.astype(BF16)
    send_ref[BOT : BOT + HALF, :] = jnp.zeros((HALF, FEAT), BF16)
    send_ref[BOT : BOT + HALF, 0:LANE] = high
    send_ref[BOT : BOT + HALF, LANE : 2 * LANE] = (sent - high.astype(F32)).astype(BF16)


def two_terms(row):
    high = row.astype(BF16).astype(F32)
    rows = lax.broadcasted_iota(jnp.int32, (HALF, LANE), 0)
    block = jnp.where(rows == 0, high, jnp.where(rows == 1, row - high, 0.0))
    return block.astype(BF16)


def paired_kernel(
    keep_a_ref, got_a_ref, keep_b_ref, got_b_ref, extra_ref, keep_sum_ref, out_ref, sum_ref
):
    total = keep_sum_ref[...]
    for start in (0, ATT):
        term = got_a_ref[ATT : ATT + HALF, start : start + ATT].astype(F32)
        total = total + term[0:1, :]
    sum_ref[0:1, :] = total[:, 0:LANE]
    sum_ref[1:2, :] = total[:, LANE : 2 * LANE]
    sum_ref[2:8, :] = jnp.zeros((6, LANE), F32)
    for p in range(N_PLANE):
        at = slice(HALF * p, HALF * (p + 1))
        for j in range(BLOCKS):
            lanes = slice(LANE * j, LANE * (j + 1))
            sum_a = keep_a_ref[at, lanes] + got_a_ref[at, lanes].astype(F32)
            sum_b = keep_b_ref[at, lanes] + got_b_ref[at, lanes].astype(F32)
            out_ref[p, PIECE * j : PIECE * j + HALF, :] = sum_a.astype(BF16)
            out_ref[p, PIECE * j + HALF : PIECE * (j + 1), :] = sum_b.astype(BF16)
        cols = slice(0, LANE), slice(LANE, 2 * LANE)
        small = extra_ref[p : p + 1, :]
        for col in cols:
            small = small + got_b_ref[BOT : BOT + HALF, col].astype(F32)[p : p + 1, :]
        out_ref[p, MAIN:TALL, :] = two_terms(small)


def small_row(block):
    return block[MAIN : MAIN + 1, :].astype(F32) + block[MAIN + 1 : MAIN + 2, :].astype(F32)


def tail_parts(ref):
    tail = ref[MAIN:TALL, :].astype(F32)
    return tail[0:1] + tail[1:2], tail[2:10], tail[10:12] + tail[12:14]


def tail_block(small, profile, sums):
    high = small.astype(BF16).astype(F32)
    sums_high = sums.astype(BF16).astype(F32)
    rows = [high, small - high, profile, sums_high, sums - sums_high, jnp.zeros((2, LANE), F32)]
    return jnp.concatenate(rows, axis=0).astype(BF16)


def plane_sum_kernel(got_ref, profile_ref, sum_ref, out_ref):
    total = got_ref[0].astype(F32)
    for p in range(1, N_PLANE):
        total = total + got_ref[p].astype(F32)
    out_ref[0:MAIN, :] = total[0:MAIN].astype(BF16)
    out_ref[MAIN:TALL, :] = tail_block(small_row(total), profile_ref[...], sum_ref[0:2, :])


def z_pair_kernel(mine_ref, other_ref, out_ref):
    total = mine_ref[0:MAIN, :].astype(F32) + other_ref[0:MAIN, :].astype(F32)
    out_ref[0:MAIN, :] = total.astype(BF16)
    small, profile, sums = tail_parts(mine_ref)
    small_o, _, sums_o = tail_parts(other_ref)
    out_ref[MAIN:TALL, :] = tail_block(small + small_o, profile, sums + sums_o)


def z_sum_kernel(mine_ref, near_ref, cross_ref, far_ref, out_ref):
    near = mine_ref[0:MAIN, :].astype(F32) + near_ref[0:MAIN, :].astype(F32)
    far = far_ref[0:MAIN, :].astype(F32) + cross_ref[0:MAIN, :].astype(F32)
    main = (near + far).astype(BF16)
    small, profile, sums = tail_parts(mine_ref)
    small_n, _, sums_n = tail_parts(near_ref)
    small_f, _, sums_f = tail_parts(far_ref)
    small_c, _, sums_c = tail_parts(cross_ref)
    small = (small + small_n) + (small_f + small_c)
    tail = tail_block(small, profile, (sums + sums_n) + (sums_f + sums_c))
    for p in range(N_PLANE):
        out_ref[p, 0:MAIN, :] = main
        out_ref[p, MAIN:TALL, :] = tail


def unpack_kernel(own, got_ref, *refs):
    up_hbm, down_hbm, v_hbm, u_hbm, gup_hbm, gdown_hbm, aw_hbm = refs[-14:-7]
    attn_ref, down_ref, up_ref, gup_ref, gdown_ref, aw_ref, sems = refs[-7:]
    first = (lax.axis_index("core") == 0) if own else (lax.axis_index("core") != 0)

    def halves(src, dst, sem):
        rows = src.shape[0] // 2
        cuts = [pl.ds(rows * h, rows) for h in range(2)]
        return [
            pltpu.make_async_copy(src.at[cut, :], dst.at[cut, :], sems.at[sem + h])
            for h, cut in enumerate(cuts)
        ]

    to_v = halves(attn_ref, v_hbm, 5)
    to_u = halves(attn_ref, u_hbm, 5)
    to_down = halves(down_ref, down_hbm, 0)
    to_up = halves(up_ref, up_hbm, 0)
    smalls = [
        pltpu.make_async_copy(gup_ref, gup_hbm, sems.at[2]),
        pltpu.make_async_copy(gdown_ref, gdown_hbm, sems.at[3]),
        pltpu.make_async_copy(aw_ref, aw_hbm, sems.at[4]),
    ]
    tails = [got_ref[p, MAIN:TALL, :].astype(F32) for p in range(N_PLANE)]
    sums = [tail[10:12] + tail[12:14] for tail in tails]
    sums = [jnp.concatenate([v[0:1], v[1:2]], axis=1) for v in sums]
    sums = jnp.concatenate(split3(jnp.concatenate(sums, axis=0)), axis=0)
    for j in range(BLOCKS):
        rows = slice(PIECE * j, PIECE * j + HALF)
        attn = got_ref[:, rows, :].astype(F32).reshape(ATT, LANE)
        profile = jnp.concatenate([tail[2 + j : 3 + j] for tail in tails], axis=0).astype(BF16)
        outer = tn(jnp.concatenate([profile, profile, profile], axis=0), sums)
        attn_ref[LANE * j : LANE * (j + 1), :] = attn.T + outer
        if j % 4 == 3:

            @pl.when(first)
            def _():
                to_v[j // 4].start()

            @pl.when(jnp.logical_not(first))
            def _():
                to_u[j // 4].start()

    @pl.when(first)
    def _():
        for h in range(2):
            pieces = slice(N_PLANE // 2 * h, N_PLANE // 2 * (h + 1))
            at = slice(BOT // 2 * h, BOT // 2 * (h + 1))
            for j in range(BLOCKS):
                rows = slice(PIECE * j + HALF, PIECE * (j + 1))
                enc = got_ref[pieces, rows, :].astype(F32).reshape(BOT // 2, LANE)
                down_ref[at, LANE * j : LANE * (j + 1)] = enc
            to_down[h].start()
        for r in range(12):
            block = got_ref[r, MAIN:TALL, :].astype(F32)
            small = block[0:1, :] + block[1:2, :]
            if r < 8:
                gdown_ref[:, LANE * r : LANE * (r + 1)] = small
            elif r < 10:
                aw_ref[:, LANE * (r - 8) : LANE * (r - 7)] = small
            else:
                gup_ref[:, LANE * (r - 10) : LANE * (r - 9)] = small
        for copy in smalls:
            copy.start()
        for copy in to_v + to_down + smalls:
            copy.wait()

    @pl.when(jnp.logical_not(first))
    def _():
        for h in range(2):
            for j in range(4 * h, 4 * h + 4):
                rows = slice(PIECE * j + HALF, PIECE * (j + 1))
                enc = got_ref[:, rows, :].astype(F32).reshape(BOT, LANE)
                up_ref[LANE * j : LANE * (j + 1), :] = enc.T
            to_up[h].start()
        for copy in to_u + to_up:
            copy.wait()


def whole_spec(shape):
    return pl.BlockSpec(shape, lambda *_: (0,) * len(shape))


def call(body, outs, *args, name):
    return pl.pallas_call(
        body,
        out_shape=[jax.ShapeDtypeStruct(s, d) for s, d in outs],
        compiler_params=params(),
        name=name,
    )(*args)


def swap(v, axis):
    return lax.ppermute(v, axis, [(0, 1), (1, 0)])


def in_hbm(*arrays):
    return [pltpu.with_memory_space_constraint(v, pltpu.HBM) for v in arrays]


def reduce_all(keep_a, got_a, keep_b, got_b, extra, keep_sum, profile):
    pieces = (N_PLANE, TALL, LANE)
    paired, sums = call(
        paired_kernel,
        [(pieces, BF16), ((8, LANE), F32)],
        keep_a, got_a, keep_b, got_b, extra, keep_sum,
        name="paired",
    )
    got = lax.all_to_all(paired, PLANE, 0, 0, tiled=True)
    flat = [(pieces[1:], BF16)]
    (part,) = call(plane_sum_kernel, flat, got, profile, sums, name="plane_sum")
    (pair,) = call(z_pair_kernel, flat, part, cross_z(part, 1), name="z_pair")
    near, cross, far = [cross_z(pair, bits) for bits in (2, 6, 4)]
    (whole,) = call(
        z_sum_kernel,
        [(pieces, BF16)],
        pair, near, cross, far,
        name="z_sum",
    )
    return lax.all_to_all(whole, PLANE, 0, 0, tiled=True)


def cross_z(v, bits):
    return lax.ppermute(v, "z", [(i, i ^ bits) for i in range(N_Z)])


def unpack(got, *before):
    hbm = pl.BlockSpec(memory_space=pltpu.HBM)
    shapes = [
        (FEAT, BOT), (BOT, FEAT), (FEAT, ATT), (FEAT, ATT), (1, BOT), (1, FEAT), (1, ATT)
    ]
    return pl.pallas_call(
        functools.partial(unpack_kernel, not before),
        in_specs=[VMEM] + [hbm] * len(before),
        out_specs=[hbm] * len(shapes),
        out_shape=[jax.ShapeDtypeStruct(v, F32) for v in shapes],
        input_output_aliases={1 + i: i for i in range(len(before))},
        scratch_shapes=[
            pltpu.VMEM((FEAT, ATT), F32),
            pltpu.VMEM((BOT, FEAT), F32),
            pltpu.VMEM((FEAT, BOT), F32),
            pltpu.VMEM((1, BOT), F32),
            pltpu.VMEM((1, FEAT), F32),
            pltpu.VMEM((1, ATT), F32),
            pltpu.SemaphoreType.DMA((7,)),
        ],
        compiler_params=params(),
        name="unpack_other" if before else "unpack_own",
    )(got, *before)


def encode(
    rows, slide_ids, counts, pooled_cot, w_up, w_down, gu, gd, attn_v, attn_u, aw
):
    hbm = pl.BlockSpec(memory_space=pltpu.HBM)
    outs = [
        ((SLOTS * POS, FEAT), BF16),
        ((SLOTS * POS, BOT), BF16),
        ((SLOTS * POS, BOT), F32),
        ((SLOTS, FEAT), F32),
        ((SLOTS, ATT), F32),
        ((SLOTS, ATT), F32),
        ((SLOTS, LANE), F32),
        ((40, LANE), F32),
        ((1, SLOTS), jnp.int32),
        ((BOT, FEAT), BF16),
        ((1, BOT), F32),
        ((1, FEAT), F32),
        ((FEAT, ATT), BF16),
        ((FEAT, ATT), BF16),
        ((1, ATT), F32),
    ]
    return pl.pallas_call(
        forward_kernel,
        in_specs=[hbm] * 10 + [pl.BlockSpec(memory_space=pltpu.SMEM)],
        out_specs=[VMEM] * len(outs),
        out_shape=[jax.ShapeDtypeStruct(s, d) for s, d in outs],
        scratch_shapes=[
            pltpu.VMEM((FEAT, BOT), BF16),
            pltpu.VMEM((1, SLOTS), jnp.int32),
            pltpu.VMEM((4, 32), BF16),
            pltpu.SemaphoreType.DMA((len(LOADS) + 9,)),
        ],
        compiler_params=params(),
        name="encode",
    )(*in_hbm(rows, w_up, w_down, gu, gd, attn_v, attn_u, aw, slide_ids, pooled_cot), counts)


def backward_rows(mask, up, back, small, w_down, gu):
    outs = [((SLOTS * POS, FEAT), BF16), ((SLOTS * POS, BOT), BF16), ((HALF, LANE), F32)]
    return call(rows_kernel, outs, mask, up, back, small, w_down, gu, name="backward_rows")


def backward_sums(x, hid, dback, dup, small):
    outs = [((BOT, FEAT), F32), ((BOT + HALF, FEAT), BF16), ((HALF, LANE), F32)]
    return call(sums_kernel, outs, x, hid, dback, dup, small, name="backward_sums")


def per_device(
    tiles, counts, slide_ids, pooled_cot, w_up, w_down, gain_up, gain_down, attn_v, attn_u, attn_w
):
    rows = tiles.reshape(SLOTS * POS, FEAT)
    gu = gain_up.reshape(1, BOT)
    gd = gain_down.reshape(1, FEAT)
    aw = attn_w.reshape(1, ATT)
    x, hid, up, feat, tanh, sigm, weight, pack, ids, *loaded = encode(
        rows, slide_ids, counts, pooled_cot, w_up, w_down, gu, gd, attn_v, attn_u, aw
    )
    w_down, gu, gd, attn_v, attn_u, aw = loaded
    (half,) = call(pair_kernel, [((40, LANE), F32)], pack, swap(pack, "core"), name="pair")
    mask, act, slope = call(
        keep_kernel,
        [((SLOTS * POS, FEAT), BF16), ((SLOTS, FEAT), F32), ((SLOTS, FEAT), F32)],
        x, hid, w_down, gd, tanh, sigm, aw, attn_v, attn_u,
        name="keep",
    )
    across, mask, act, slope = lax.optimization_barrier((swap(half, "x_hi"), mask, act, slope))
    (spread,) = call(spread_kernel, [((N_Z, 40, LANE), F32)], half, across, name="spread")
    got = lax.all_to_all(spread, "z", 0, 0, tiled=True)

    back, pooled, small, keep_a, send_a, keep_sum, profile = pl.pallas_call(
        middle_kernel,
        in_specs=[VMEM] * 10,
        out_shape=[
            jax.ShapeDtypeStruct((SLOTS, FEAT), F32),
            jax.ShapeDtypeStruct((4, FEAT), F32),
            jax.ShapeDtypeStruct((16, LANE), F32),
            jax.ShapeDtypeStruct((ATT, FEAT), F32),
            jax.ShapeDtypeStruct((ATT + HALF, FEAT), BF16),
            jax.ShapeDtypeStruct((1, ATT), F32),
            jax.ShapeDtypeStruct((8, LANE), F32),
        ],
        compiler_params=params(),
        name="middle",
    )(ids, got, feat, act, slope, tanh, sigm, weight, aw, gd)

    dback, dup, small = backward_rows(mask, up, back, small, w_down, gu)
    got_a, dback = lax.optimization_barrier((swap(send_a, "core"), dback))
    keep_b, send_b, extra = backward_sums(x, hid, dback, dup, small)
    got_b = swap(send_b, "core")

    mine = reduce_all(keep_a, got_a, keep_b, got_b, extra, keep_sum, profile)
    other = swap(mine, "core")
    g_up, g_down, g_v, g_u, g_gu, g_gd, g_aw = unpack(other, *unpack(mine))
    return (
        pooled,
        g_up,
        g_down,
        g_gu.reshape(BOT),
        g_gd.reshape(FEAT),
        g_v,
        g_u,
        g_aw.reshape(ATT),
    )


def solution(mesh):
    fine = Mesh(mesh.devices.reshape(2, 4, 2, 8, 2), FINE)
    return jax.shard_map(
        per_device,
        mesh=fine,
        in_specs=(
            P(SLIDE, TILE, None, None),
            P(SLIDE, TILE),
            P(SLIDE, TILE),
            P(SLIDE, TILE),
            P(),
            P(),
            P(),
            P(),
            P(),
            P(),
            P(),
        ),
        out_specs=(P(SLIDE, None), P(), P(), P(), P(), P(), P(), P()),
        check_vma=False,
    )
```
